128 devices in a mesh: orb: 32 (over y, x, core), grid: 4 (over z).
Axes of the slice: x: 4, y: 4, z: 4, core: 2. Of those that a mesh axis runs over, the one named last changes fastest.
Arguments:
- orbitals: bfloat16 [1024, 40, 1600], P('orb', 'grid')
- box_offset: int32 [1024, 3], replicated, may hold values from 0 to 235, as said below
- partner_slot: int32 [32, 32, 4], P('orb'), may hold values from -1 to 31, as said below
- first_slot: int32 [32, 32, 4], P('orb'), may hold values from -1 to 31, as said below
Outputs:
- exchange_terms: float32 [1024, 40, 1600], P('orb', 'grid')
- gram: float32 [1024, 1024], replicated
The draws below stay inside these ranges and needn't reach their ends.
Inputs may be any that keep to these rules, and one draw needn't show every extreme that they name: `box_offset`: entries lie within 20 of one another along each of the three dimensions, and both ends of that span are reached. `partner_slot`: -1 marks an empty slot; every owner o has all 4 slots toward owner (o + 1) mod 32 live; where o equals d the two orbitals of a slot differ. `first_slot`: -1 exactly where partner_slot is -1.
All inputs are finite; a program needn't handle non-finite values.
Results may differ from the reference program's by a relative error of at most 0.0045.
The reference program's roundings to bfloat16 on the way count: a program that leaves them out, or rounds other values in their place, can miss the bound.
Values may be sent and summed in bfloat16 or wider, within the bound.
A program may use at most 192 MiB of HBM per device.

```python
import math
import jax
import jax.numpy as jnp
from jax import lax

ORB_DEV = 32
BOX = 40
CAP = 4
ORBITALS = 1024
BOXSQ = 1600
N_ORB = 32


def draw_orbitals(key, part):
    key = jax.random.fold_in(key, 11)
    scale_key, value_key = jax.random.split(key, 2)
    scales = jnp.exp(jax.random.uniform(scale_key, (ORBITALS, 1, 1), minval=math.log(0.4), maxval=math.log(2.5)))
    values = jnp.clip(jax.random.normal(value_key, (ORBITALS, BOX, BOXSQ)), -4.0, 4.0)
    return (scales * values).astype(jnp.bfloat16)


def draw_box_offset(key, part):
    key = jax.random.fold_in(key, 12)
    base_key, order_key, spread_key = jax.random.split(key, 3)
    middle = jax.random.randint(base_key, (1,), 0, 216)
    corners = jnp.concatenate([jnp.array([215, 0], dtype=jnp.int32), middle.astype(jnp.int32)])
    base = jax.random.permutation(order_key, corners)[None, :]
    spread = jax.random.randint(spread_key, (ORBITALS, 3), 0, 21)
    spread = spread.at[0].set(0).at[1].set(20)
    return (base + spread).astype(jnp.int32)


def pair_lists(key):
    live_key, first_key, partner_key, step_key = jax.random.split(key, 4)
    shape = (N_ORB, N_ORB, CAP)
    owners = jnp.arange(N_ORB)[:, None, None]
    targets = jnp.arange(N_ORB)[None, :, None]
    apart = jnp.abs(owners - targets)
    apart = jnp.minimum(apart, N_ORB - apart)
    limit = jnp.where(apart <= 1, 100, jnp.where(apart <= 3, 70, jnp.where(apart <= 7, 40, 25)))
    rolled = jax.random.randint(live_key, shape, 0, 100)
    alive = (rolled < limit) | (targets == (owners + 1) % N_ORB)
    firsts = jax.random.randint(first_key, shape, 0, ORB_DEV)
    others = jax.random.randint(partner_key, shape, 0, ORB_DEV)
    stepped = jax.random.randint(step_key, shape, 1, ORB_DEV)
    seconds = jnp.where(owners == targets, (firsts + stepped) % ORB_DEV, others)
    return (jnp.where(alive, firsts, -1).astype(jnp.int32), jnp.where(alive, seconds, -1).astype(jnp.int32))


def draw_partner_slot(key, part):
    lists = pair_lists(key)
    return lists[1]


def draw_first_slot(key, part):
    lists = pair_lists(key)
    return lists[0]


def setup_inputs(seed: int = 0) -> dict:
    keys = jax.random.split(jax.random.key(seed), 5)
    return {
        "orbitals": draw_orbitals(jax.random.fold_in(keys[4], 71), 0),
        "box_offset": draw_box_offset(jax.random.fold_in(keys[4], 71), 0),
        "partner_slot": draw_partner_slot(jax.random.fold_in(keys[4], 71), 0),
        "first_slot": draw_first_slot(jax.random.fold_in(keys[4], 71), 0),
    }


def tables(box_edge):
    wave_number = jnp.arange(box_edge, dtype=jnp.float32) + 1.0
    sine_table = jnp.sqrt(2.0 / (box_edge + 1.0)) * jnp.sin(math.pi * wave_number[:, None] * wave_number[None, :] / (box_edge + 1.0))
    plane_table = (sine_table[:, None, :, None] * sine_table[None, :, None, :]).reshape(box_edge * box_edge, box_edge * box_edge).astype(jnp.bfloat16)
    eigen_one = 2.0 - 2.0 * jnp.cos(math.pi * wave_number / (box_edge + 1.0))
    eigen_sum = eigen_one[:, None, None] + eigen_one[None, :, None] + eigen_one[None, None, :]
    green_table = (1.0 / eigen_sum).reshape(box_edge, box_edge * box_edge)
    return (sine_table, plane_table, green_table)

def moved(source, delta):
    box_edge = source.shape[0]
    cubic = source.reshape(box_edge, box_edge, box_edge)
    cells = jnp.arange(box_edge, dtype=jnp.int32)
    along_x = cells + delta[0]
    along_y = cells + delta[1]
    along_z = cells + delta[2]

    def within(where_to):
        return (where_to >= 0) & (where_to < box_edge)
    inside = within(along_x)[:, None, None] & within(along_y)[None, :, None] & within(along_z)[None, None, :]
    cubic = jnp.take(cubic, jnp.clip(along_x, 0, box_edge - 1), axis=0)
    cubic = jnp.take(cubic, jnp.clip(along_y, 0, box_edge - 1), axis=1)
    cubic = jnp.take(cubic, jnp.clip(along_z, 0, box_edge - 1), axis=2)
    return jnp.where(inside, cubic, jnp.zeros((), source.dtype)).reshape(box_edge, box_edge * box_edge)

def pair_terms(phi_first, phi_second, delta, sine_table, plane_table, green_table):
    box_edge = phi_first.shape[0]
    shifted = moved(phi_second, delta)
    density = phi_first.astype(jnp.float32) * shifted.astype(jnp.float32)
    forward = jnp.dot(sine_table, density, precision=lax.Precision.HIGHEST).astype(jnp.bfloat16)
    coeffs = jnp.dot(forward, plane_table, preferred_element_type=jnp.float32)
    scaled = (green_table * coeffs).astype(jnp.bfloat16)
    inverse = jnp.dot(scaled, plane_table, preferred_element_type=jnp.float32)
    potential = jnp.dot(sine_table, inverse, precision=lax.Precision.HIGHEST)
    energy = jnp.sum(density * potential) / (box_edge * box_edge * box_edge)
    own_term = potential * shifted.astype(jnp.float32)
    product = (potential * phi_first.astype(jnp.float32)).astype(jnp.bfloat16)
    returned = moved(product, -delta)
    return (own_term, returned, energy)

def reference(orbitals, box_offset, partner_slot, first_slot):
    box_edge = orbitals.shape[1]
    orbital_count = orbitals.shape[0]
    sine_table, plane_table, green_table = tables(box_edge)
    owners = jnp.broadcast_to(jnp.arange(N_ORB, dtype=jnp.int32)[:, None, None], partner_slot.shape)
    partner_owners = jnp.broadcast_to(jnp.arange(N_ORB, dtype=jnp.int32)[None, :, None], partner_slot.shape)
    alive_slots = (partner_slot >= 0).reshape(-1)
    first_global = (owners * ORB_DEV + jnp.maximum(first_slot, 0)).reshape(-1).astype(jnp.int32)
    second_global = (partner_owners * ORB_DEV + jnp.maximum(partner_slot, 0)).reshape(-1).astype(jnp.int32)

    def visit(running, slot_data):
        terms, gram = running
        first_id, second_id, alive = slot_data
        delta = box_offset[first_id] - box_offset[second_id]
        own_term, returned, energy = pair_terms(orbitals[first_id], orbitals[second_id], delta, sine_table, plane_table, green_table)
        weight = jnp.where(alive, jnp.float32(1.0), jnp.float32(0.0))
        terms = terms.at[first_id].add(weight * own_term)
        terms = terms.at[second_id].add(weight * returned.astype(jnp.float32))
        gram = gram.at[first_id, second_id].add(weight * energy)
        gram = gram.at[second_id, first_id].add(weight * energy)
        return ((terms, gram), None)
    start = (jnp.zeros(orbitals.shape, jnp.float32), jnp.zeros((orbital_count, orbital_count), jnp.float32))
    (terms, gram), unused = lax.scan(visit, start, (first_global, second_global, alive_slots))
    return (terms, gram)
```

```python
import functools
import math

import jax
import jax.numpy as jnp
import ml_dtypes
import numpy as np
from jax import lax
from jax.experimental import pallas as pl
from jax.experimental.pallas import tpu as pltpu
from jax.sharding import PartitionSpec as P

BF16 = jnp.bfloat16
F32 = jnp.float32
VMEM = pl.BlockSpec(memory_space=pltpu.VMEM)
SMEM = pl.BlockSpec(memory_space=pltpu.SMEM)
EDGE = 40
AREA = 1600
ORB_DEV = 32
CAP = 4
SLOTS = 32
BATCH = 8
PADDED = 1792
TOP = 24
LEFT = 896
TILES = [(at, min(128, AREA - at)) for at in range(0, AREA, 128)]
WIDE = [(at, min(256, AREA - at)) for at in range(0, AREA, 256)]


@functools.cache
def tables():
    number = np.arange(EDGE, dtype=np.float64) + 1.0
    sine = np.sqrt(2.0 / (EDGE + 1.0)) * np.sin(
        math.pi * number[:, None] * number[None, :] / (EDGE + 1.0)
    )
    sine32 = sine.astype(np.float32)
    plane = (sine32[:, None, :, None] * sine32[None, :, None, :]).reshape(AREA, AREA)
    plane = np.pad(plane, ((0, 0), (0, PADDED - AREA))).astype(ml_dtypes.bfloat16)
    eigen = 2.0 - 2.0 * np.cos(math.pi * number / (EDGE + 1.0))
    green = 1.0 / (eigen[:, None, None] + eigen[None, :, None] + eigen[None, None, :])
    green = np.pad(green.reshape(EDGE, AREA), ((0, 0), (0, PADDED - AREA)))
    green = np.tile(green.astype(np.float32), (2, 1))
    high = sine32.astype(ml_dtypes.bfloat16)
    low = (sine32 - high.astype(np.float32)).astype(ml_dtypes.bfloat16)
    two = np.eye(2, dtype=np.float32)
    pair_high = np.kron(two, high.astype(np.float32))
    pair_low = np.kron(two, low.astype(np.float32))
    sine_pair = np.concatenate([pair_high, pair_high, pair_low], 1).astype(ml_dtypes.bfloat16)
    along_z = np.tile(np.arange(1664, dtype=np.int32) % EDGE, (8, 1))
    return sine_pair, plane, green, along_z


def selector(index_of):
    column = lax.broadcasted_iota(jnp.int32, (8, 256), 1)
    row = lax.broadcasted_iota(jnp.int32, (8, 256), 0)
    offset = column - row * ORB_DEV
    blocks = []
    for slot in range(SLOTS):
        index = index_of(slot)
        index = jnp.where(index < 0, 100000, index)
        blocks.append((offset == index).astype(F32))
    return jnp.concatenate(blocks, 0)


def pick_kernel(place, partner, first, own, picked, phi):
    me, level = place[0], place[1]
    sel_picked = selector(lambda s: partner[s * 128 + me * CAP + level]).astype(BF16)
    sel_phi = selector(lambda s: first[me * 128 + s * CAP + level]).astype(BF16)
    both = jnp.concatenate([sel_picked, sel_phi], 0)
    for at, width in WIDE:
        cols = slice(at, at + width)
        for start in range(0, EDGE, 16):
            parts = []
            for chunk in range(start, min(start + 16, EDGE), 8):
                source = own[chunk : chunk + 8, :, cols].reshape(256, width)
                out = jnp.dot(both, source, preferred_element_type=F32)
                parts.append(out.reshape(2 * SLOTS, 8, width))
            out = jnp.concatenate(parts, 1).astype(BF16)
            rows = slice(start, start + out.shape[1])
            picked[:, rows, cols] = out[:SLOTS]
            phi[:, rows, cols] = out[SLOTS:]


def shift_tiles(pad, along_z, deltas, emit):
    dx, dy, dz = deltas
    start = LEFT + EDGE * dy + dz
    whole = lax.div(start, 128)
    part = start - whole * 128
    turn = lax.rem(128 - part, 128)
    lane = lax.broadcasted_iota(jnp.int32, (EDGE, 128), 1)
    from_here = lane < 128 - part
    rows = pl.ds(TOP + dx, EDGE)

    def turned(tile):
        return pltpu.roll(pad[whole + tile, rows, :], turn, 1)

    here = turned(0)
    for tile, (at, width) in enumerate(TILES):
        after = turned(tile + 1)
        out = jnp.where(from_here, here, after)
        z = along_z[:, at : at + 128] + dz
        inside = (z >= 0) & (z < EDGE)
        out = jnp.where(inside[None], out.reshape(EDGE // 8, 8, 128), 0.0).reshape(EDGE, 128)
        emit(at, width, out)
        here = after


def solve_kernel(
    place, partner, first, offset, partners, phis, sine_pair, plane, green, along_z,
    returned, own_terms, energies,
    live, pad, den, stack, forward, scaled, inverse, shifted, potential,
):
    me, level = place[0], place[1]

    def compact(slot, count):
        alive = partner[me * 128 + slot * CAP + level] >= 0
        energies[slot] = 0.0

        @pl.when(alive)
        def _():
            live[count] = slot

        @pl.when(jnp.logical_not(alive))
        def _():
            returned[slot] = jnp.zeros((EDGE, AREA), BF16)
            own_terms[slot] = jnp.zeros((EDGE, AREA), BF16)

        return count + alive.astype(jnp.int32)

    count = lax.fori_loop(0, SLOTS, compact, jnp.int32(0))
    pad[...] = jnp.zeros_like(pad)
    den[...] = jnp.zeros_like(den)

    def deltas_of(slot):
        at = me * 128 + slot * CAP + level
        i = (me * ORB_DEV + first[at]) * 3
        j = (slot * ORB_DEV + partner[at]) * 3
        return tuple(offset[i + axis] - offset[j + axis] for axis in range(3))

    def split(value):
        high = value.astype(BF16)
        return high, (value - high.astype(F32)).astype(BF16)

    def sine_product(cols):
        return jnp.dot(sine_pair[...], stack[:, cols], preferred_element_type=F32)

    def batch(index, _):
        base = index * BATCH
        pairs = lax.div(jnp.minimum(count - base, BATCH) + 1, 2)

        def before(pair, _):
            for side in range(2):
                position = base + pair * 2 + side
                rows = pl.ds(pl.multiple_of(pair * 80 + side * EDGE, 8), EDGE)

                @pl.when(position < count)
                def _():
                    slot = live[position]
                    for at, width in TILES:
                        pad[(LEFT + at) // 128, TOP : TOP + EDGE, :width] = partners[
                            slot, :, at : at + width
                        ].astype(F32)

                    def emit(at, width, out):
                        shifted[rows, at : at + 128] = out
                        phi = phis[slot, :, at : at + width].astype(F32)
                        den[side * EDGE : (side + 1) * EDGE, at : at + width] = (
                            phi * out[:, :width]
                        )

                    shift_tiles(pad, along_z, deltas_of(slot), emit)

            for at, width in TILES:
                cols = slice(at, at + width)
                high, low = split(den[:, cols])
                stack[0:80, cols] = high
                stack[80:160, cols] = low
                stack[160:240, cols] = high
            rows = pl.ds(pl.multiple_of(pair * 80, 16), 80)
            for at, width in WIDE:
                cols = slice(at, at + width)
                forward[rows, cols] = sine_product(cols).astype(BF16)
            return 0

        lax.fori_loop(0, pairs, before, 0)

        def to_coeffs(step, _):
            cols = pl.ds(pl.multiple_of(step * 256, 256), 256)
            coeffs = jnp.dot(forward[...], plane[:, cols], preferred_element_type=F32)
            for pair in range(BATCH // 2):
                scaled[pair * 80 : pair * 80 + 80, cols] = (
                    green[:, cols] * coeffs[pair * 80 : pair * 80 + 80]
                ).astype(BF16)
            return 0

        lax.fori_loop(0, PADDED // 256, to_coeffs, 0)

        def to_inverse(step, _):
            cols = pl.ds(pl.multiple_of(step * 256, 256), 256)
            inverse[:, cols] = jnp.dot(
                scaled[:, :AREA], plane[:, cols], preferred_element_type=F32
            )
            return 0

        lax.fori_loop(0, PADDED // 256, to_inverse, 0)

        def after(pair, _):
            rows = pl.ds(pl.multiple_of(pair * 80, 16), 80)
            for at, width in TILES:
                cols = slice(at, at + width)
                high, low = split(inverse[rows, cols])
                stack[0:80, cols] = high
                stack[80:160, cols] = low
                stack[160:240, cols] = high
            for at, width in WIDE:
                cols = slice(at, at + width)
                potential[:, cols] = sine_product(cols)
            for side in range(2):
                position = base + pair * 2 + side
                half = pl.ds(pl.multiple_of(pair * 80 + side * EDGE, 8), EDGE)

                @pl.when(position < count)
                def _():
                    slot = live[position]
                    energy = jnp.zeros((EDGE, 128), F32)
                    for at, width in TILES:
                        cols = slice(at, at + width)
                        phi = phis[slot, :, cols].astype(F32)
                        solved = potential[side * EDGE : (side + 1) * EDGE, cols]
                        term = solved * shifted[half, cols]
                        own_terms[slot, :, cols] = term.astype(BF16)
                        cell = term * phi
                        if width < 128:
                            cell = jnp.concatenate(
                                [cell, jnp.zeros((EDGE, 128 - width), F32)], 1
                            )
                        energy = energy + cell
                        pad[(LEFT + at) // 128, TOP : TOP + EDGE, :width] = (
                            (solved * phi).astype(BF16).astype(F32)
                        )
                    energies[slot] = jnp.sum(energy) / (EDGE * EDGE * EDGE)

                    back = tuple(-delta for delta in deltas_of(slot))

                    def emit(at, width, out):
                        returned[slot, :, at : at + width] = out[:, :width].astype(BF16)

                    shift_tiles(pad, along_z, back, emit)

            return 0

        lax.fori_loop(0, pairs, after, 0)
        return 0

    lax.fori_loop(0, lax.div(count + BATCH - 1, BATCH), batch, 0)


def sum_kernel(place, partner, first, returned, own_terms, total):
    me, level = place[0], place[1]
    back = selector(lambda s: partner[s * 128 + me * CAP + level]).T.astype(BF16)
    ahead = selector(lambda s: first[me * 128 + s * CAP + level]).T.astype(BF16)
    for at, width in WIDE:
        cols = slice(at, at + width)
        for start in range(0, EDGE, 16):
            stop = min(start + 16, EDGE)
            boxes = returned[:, start:stop, cols].astype(F32)
            terms = own_terms[:, start:stop, cols].astype(F32)
            for chunk in range(start, stop, 8):
                part = slice(chunk - start, chunk - start + 8)
                out = jnp.dot(
                    back,
                    boxes[:, part].reshape(256, width).astype(BF16),
                    preferred_element_type=F32,
                ) + jnp.dot(
                    ahead,
                    terms[:, part].reshape(256, width).astype(BF16),
                    preferred_element_type=F32,
                )
                total[chunk : chunk + 8, :, cols] = out.reshape(8, ORB_DEV, width).astype(
                    BF16
                )


def gram_kernel(partner, first, energy, gram, half):
    orbitals = gram.shape[0]
    row = lax.broadcasted_iota(jnp.int32, (orbitals, 128), 0)
    slot = lax.broadcasted_iota(jnp.int32, (orbitals, 128), 1)
    owner_here = lax.div(row, ORB_DEV) == lax.div(slot, CAP)
    within = lax.rem(row, ORB_DEV)
    first_row = lax.broadcasted_iota(jnp.int32, (ORB_DEV, 128), 0)

    def owner(index, _):
        here = pl.ds(index, 1)
        second = (owner_here & (within == partner[here, :])).astype(F32).astype(BF16)
        value = jnp.where(first_row == first[here, :], energy[here, :], 0.0)
        high = value.astype(BF16)
        rest = value - high.astype(F32)
        middle = rest.astype(BF16)
        low = (rest - middle.astype(F32)).astype(BF16)
        parts = jnp.concatenate([high, middle, low], 0)
        out = lax.dot_general(
            parts, second, (((1,), (1,)), ((), ())), preferred_element_type=F32
        )
        rows = pl.ds(pl.multiple_of(index * ORB_DEV, ORB_DEV), ORB_DEV)
        half[rows, :] = out[0:32] + out[32:64] + out[64:96]
        return 0

    lax.fori_loop(0, orbitals // ORB_DEV, owner, 0)
    for y in range(0, orbitals, 128):
        for x in range(0, orbitals, 128):
            gram[y : y + 128, x : x + 128] = (
                half[y : y + 128, x : x + 128] + half[x : x + 128, y : y + 128].T
            )


def params(mebibytes, **more):
    return pltpu.CompilerParams(vmem_limit_bytes=mebibytes * 2**20, **more)


BOXES = jax.ShapeDtypeStruct((SLOTS, EDGE, AREA), BF16)


def pick(place, partner, first, own):
    return pl.pallas_call(
        pick_kernel,
        out_shape=(BOXES, BOXES),
        in_specs=[SMEM, SMEM, SMEM, VMEM],
        out_specs=(VMEM, VMEM),
        compiler_params=params(48),
        name="pick",
    )(place, partner, first, own)


def solve(place, partner, first, offset, partners, phis):
    constants = [jnp.asarray(table) for table in tables()]
    return pl.pallas_call(
        solve_kernel,
        out_shape=(BOXES, BOXES, jax.ShapeDtypeStruct((SLOTS,), F32)),
        in_specs=[SMEM] * 4 + [VMEM] * 6,
        out_specs=(VMEM, VMEM, SMEM),
        scratch_shapes=[
            pltpu.SMEM((SLOTS + 8,), jnp.int32),
            pltpu.VMEM((27, 88, 128), F32),
            pltpu.VMEM((80, 1664), F32),
            pltpu.VMEM((240, AREA), BF16),
            pltpu.VMEM((BATCH * EDGE, AREA), BF16),
            pltpu.VMEM((BATCH * EDGE, PADDED), BF16),
            pltpu.VMEM((BATCH * EDGE, PADDED), F32),
            pltpu.VMEM((BATCH * EDGE, 1664), F32),
            pltpu.VMEM((80, AREA), F32),
        ],
        compiler_params=params(58),
        name="solve",
    )(place, partner, first, offset, partners, phis, *constants)


def sum_terms(place, partner, first, returned, own_terms):
    return pl.pallas_call(
        sum_kernel,
        out_shape=jax.ShapeDtypeStruct((EDGE, ORB_DEV, AREA), BF16),
        in_specs=[SMEM] * 3 + [VMEM] * 2,
        out_specs=VMEM,
        compiler_params=params(48),
        name="sum_terms",
    )(place, partner, first, returned, own_terms)


def gram_of(partner, first, energy, orbitals):
    return pl.pallas_call(
        gram_kernel,
        out_shape=jax.ShapeDtypeStruct((orbitals, orbitals), F32),
        in_specs=[VMEM] * 3,
        out_specs=VMEM,
        scratch_shapes=[pltpu.VMEM((orbitals, orbitals), F32)],
        compiler_params=params(32),
        name="gram",
    )(partner, first, energy)


def on_device(orbitals, box_offset, partner_slot, first_slot):
    orb_count = lax.axis_size("orb")
    place = jnp.stack([lax.axis_index("orb"), lax.axis_index("grid")]).astype(jnp.int32)
    own = lax.all_gather(orbitals.transpose(1, 0, 2), "grid", axis=0, tiled=True)
    lists = lax.all_gather(
        jnp.concatenate([partner_slot, first_slot], 0).reshape(1, 2, -1), "orb", tiled=True
    )
    partner_rows, first_rows = lists[:, 0], lists[:, 1]
    partner, first = partner_rows.reshape(-1), first_rows.reshape(-1)
    picked, phis = pick(place, partner, first, own)
    partners = lax.all_to_all(picked, "orb", split_axis=0, concat_axis=0, tiled=True)
    products, own_terms, energies = solve(
        place, partner, first, box_offset.reshape(-1), partners, phis
    )
    returned = lax.all_to_all(products, "orb", split_axis=0, concat_axis=0, tiled=True)
    shared = lax.all_gather(energies, ("orb", "grid"))
    shared = shared.reshape(orb_count, CAP, orb_count).transpose(0, 2, 1)
    gram = gram_of(
        partner_rows, first_rows, shared.reshape(orb_count, -1), orb_count * ORB_DEV
    )
    total = sum_terms(place, partner, first, returned, own_terms)
    terms = lax.psum_scatter(total, "grid", scatter_dimension=0, tiled=True)
    return (terms.astype(F32).transpose(1, 0, 2), gram)


def solution(mesh):
    placed = (P("orb", "grid", None), P(), P("orb", None, None), P("orb", None, None))
    return jax.shard_map(
        on_device,
        mesh=mesh,
        in_specs=placed,
        out_specs=(P("orb", "grid", None), P()),
        check_vma=False,
    )
```

```python
import functools
import math

import jax
import jax.numpy as jnp
import ml_dtypes
import numpy as np
from jax import lax
from jax.experimental import pallas as pl
from jax.experimental.pallas import tpu as pltpu
from jax.sharding import PartitionSpec as P

BF16 = jnp.bfloat16
F32 = jnp.float32
VMEM = pl.BlockSpec(memory_space=pltpu.VMEM)
SMEM = pl.BlockSpec(memory_space=pltpu.SMEM)
EDGE = 40
AREA = 1600
ORB_DEV = 32
CAP = 4
SLOTS = 32
BATCH = 8
PADDED = 1792
TOP = 24
LEFT = 896
TILES = [(at, min(128, AREA - at)) for at in range(0, AREA, 128)]
CHUNKS = [(0, 256), (256, 256), (512, 384), (896, 384), (1280, 320)]
PEERS = 8
LEVELS = 4
MESH = pl.DeviceIdType.MESH
WIDE = [(at, min(256, AREA - at)) for at in range(0, AREA, 256)]


@functools.cache
def tables():
    number = np.arange(EDGE, dtype=np.float64) + 1.0
    sine = np.sqrt(2.0 / (EDGE + 1.0)) * np.sin(
        math.pi * number[:, None] * number[None, :] / (EDGE + 1.0)
    )
    sine32 = sine.astype(np.float32)
    plane = (sine32[:, None, :, None] * sine32[None, :, None, :]).reshape(AREA, AREA)
    plane = np.pad(plane, ((0, 0), (0, PADDED - AREA))).astype(ml_dtypes.bfloat16)
    eigen = 2.0 - 2.0 * np.cos(math.pi * number / (EDGE + 1.0))
    green = 1.0 / (eigen[:, None, None] + eigen[None, :, None] + eigen[None, None, :])
    green = np.pad(green.reshape(EDGE, AREA), ((0, 0), (0, PADDED - AREA)))
    green = np.tile(green.astype(np.float32), (2, 1))
    high = sine32.astype(ml_dtypes.bfloat16)
    low = (sine32 - high.astype(np.float32)).astype(ml_dtypes.bfloat16)
    two = np.eye(2, dtype=np.float32)
    pair_high = np.kron(two, high.astype(np.float32))
    pair_low = np.kron(two, low.astype(np.float32))
    sine_pair = np.concatenate([pair_high, pair_high, pair_low], 1).astype(ml_dtypes.bfloat16)
    along_z = np.tile(np.arange(1664, dtype=np.int32) % EDGE, (8, 1))
    return sine_pair, plane, green, along_z


def offset_class(level, a):
    return level if a < 4 else 3 - level


def peer_of(me, level, a):
    kind = offset_class(level, a)
    x = lax.rem(lax.div(me, 2) + 2 * (a % 2) + lax.rem(kind, 2), 4)
    y = lax.rem(lax.div(me, 8) + 2 * (a // 2 % 2) + lax.div(kind, 2), 4)
    return y * 8 + x * 2 + lax.rem(me + a // 4, 2)


def mirror_of(level, a):
    kind = offset_class(level, a)
    x = lax.rem(a % 2 + lax.rem(kind, 2), 2)
    y = lax.rem(a // 2 % 2 + lax.div(kind, 2), 2)
    return a // 4 * 4 + y * 2 + x


def selector(index_of):
    column = lax.broadcasted_iota(jnp.int32, (8, 256), 1)
    row = lax.broadcasted_iota(jnp.int32, (8, 256), 0)
    offset = column - row * ORB_DEV
    blocks = []
    for slot in range(SLOTS):
        index = index_of(slot // CAP, slot % CAP)
        index = jnp.where(index < 0, 100000, index)
        blocks.append((offset == index).astype(F32))
    return jnp.concatenate(blocks, 0)


def entry(row, at):
    lane = lax.broadcasted_iota(jnp.int32, (1, 128), 1)
    return jnp.sum(jnp.where(lane == at, row, 0), axis=1, keepdims=True)


def selectors(me, level, lists, mine):
    asked = selector(lambda a, c: entry(lists[level, a, 0:1, :], me * CAP + c))
    ahead = selector(lambda a, c: entry(mine[1:2, :], peer_of(me, level, a) * CAP + c))
    return asked, ahead


def greet(me, level):
    barrier = pltpu.get_barrier_semaphore()
    for a in range(1, PEERS):
        pl.semaphore_signal(
            barrier, inc=1, device_id=(peer_of(me, level, a), level), device_id_type=MESH
        )
    for step in range(1, LEVELS):
        pl.semaphore_signal(
            barrier, inc=1, device_id=(me, lax.rem(level + step, LEVELS)), device_id_type=MESH
        )

    @pl.when(level != 0)
    def _():
        pl.semaphore_signal(
            barrier, inc=1, device_id=(peer_of(me, level, 0), level), device_id_type=MESH
        )
        pl.semaphore_wait(barrier, PEERS + LEVELS - 1)

    @pl.when(level == 0)
    def _():
        pl.semaphore_wait(barrier, PEERS + LEVELS - 2)


class Exchange:
    def __init__(self, me, level, source, target, send, receive):
        self.level = level
        self.local = (source(0), target(0), send.at[0])
        self.copies = [
            pltpu.make_async_remote_copy(
                source(a),
                target(mirror_of(level, a)),
                send.at[a],
                receive.at[mirror_of(level, a)],
                device_id=(peer_of(me, level, a), level),
                device_id_type=MESH,
            )
            for a in range(PEERS)
        ]
        self.arrivals = [
            pltpu.make_async_remote_copy(
                source(a),
                target(a),
                send.at[a],
                receive.at[a],
                device_id=(peer_of(me, level, a), level),
                device_id_type=MESH,
            )
            for a in range(PEERS)
        ]

    def start(self):
        @pl.when(self.level != 0)
        def _():
            self.copies[0].start()

        @pl.when(self.level == 0)
        def _():
            pltpu.make_async_copy(*self.local).start()

        for copy in self.copies[1:]:
            copy.start()

    def wait_recv(self):
        @pl.when(self.level != 0)
        def _():
            self.arrivals[0].wait_recv()

        @pl.when(self.level == 0)
        def _():
            pltpu.make_async_copy(*self.local).wait()

        for copy in self.arrivals[1:]:
            copy.wait_recv()

    def wait_send(self):
        @pl.when(self.level != 0)
        def _():
            self.copies[0].wait_send()

        for copy in self.copies[1:]:
            copy.wait_send()


class Spread:
    def __init__(self, me, level, source, target, send, receive):
        self.copies = []
        for step in range(1, LEVELS):
            other = lax.rem(level + step, LEVELS)
            self.copies.append(
                pltpu.make_async_remote_copy(
                    source(other),
                    target(level),
                    send.at[step],
                    receive.at[step],
                    device_id=(me, other),
                    device_id_type=MESH,
                )
            )
        self.arrivals = []
        for step in range(1, LEVELS):
            other = lax.rem(level + LEVELS - step, LEVELS)
            self.arrivals.append(
                pltpu.make_async_remote_copy(
                    source(other),
                    target(other),
                    send.at[step],
                    receive.at[step],
                    device_id=(me, other),
                    device_id_type=MESH,
                )
            )

    def start(self):
        for copy in self.copies:
            copy.start()

    def wait_recv(self):
        for copy in self.arrivals:
            copy.wait_recv()

    def wait_send(self):
        for copy in self.copies:
            copy.wait_send()


def fetch_kernel(mine, own, *refs):
    count = len(CHUNKS)
    partners, phis, lists = refs[:count], refs[count : 2 * count], refs[2 * count]
    refs = refs[2 * count + 1 :]
    gathered, picked = refs[:count], refs[count : 2 * count]
    peer_send, peer_receive, level_send, level_receive = refs[2 * count :]
    me, level = lax.axis_index("orb"), lax.axis_index("grid")
    greet(me, level)
    spreads, exchanges = [], []
    for k, (at, width) in enumerate(CHUNKS):
        spreads.append(
            Spread(
                me, level,
                lambda other, at=at, width=width: own.at[:, :, pl.ds(at, width)],
                lambda other, k=k: gathered[k].at[other],
                level_send.at[k], level_receive.at[k],
            )
        )
        exchanges.append(
            Exchange(
                me, level,
                lambda a, k=k: picked[k].at[pl.ds(a * CAP, CAP)],
                lambda a, k=k: partners[k].at[pl.ds(a * CAP, CAP)],
                peer_send.at[k], peer_receive.at[k],
            )
        )
    near = Exchange(
        me, level, lambda a: mine, lambda a: lists.at[level, a],
        peer_send.at[count], peer_receive.at[count],
    )
    far = Spread(
        me, level, lambda other: lists.at[level], lambda other: lists.at[other],
        level_send.at[count], level_receive.at[count],
    )
    near.start()
    for spread in spreads:
        spread.start()
    for k, (at, width) in enumerate(CHUNKS):
        gathered[k][level] = own[:, :, at : at + width]
    near.wait_recv()
    far.start()
    asked, ahead = selectors(me, level, lists, mine)
    both = jnp.concatenate([asked, ahead], 0).astype(BF16)
    for k, (at, width) in enumerate(CHUNKS):
        spreads[k].wait_recv()
        planes = gathered[k].reshape(EDGE, ORB_DEV, width)
        for start in range(0, EDGE, 8):
            source = planes[start : start + 8].reshape(256, width)
            out = jnp.dot(both, source, preferred_element_type=F32).astype(BF16)
            out = out.reshape(2 * SLOTS, 8, width)
            picked[k][:, start : start + 8, :] = out[:SLOTS]
            phis[k][:, start : start + 8, :] = out[SLOTS:]
        exchanges[k].start()
    far.wait_recv()
    for exchange in exchanges:
        exchange.wait_recv()
    for part in [near, far] + spreads + exchanges:
        part.wait_send()


def give_back_kernel(mine, lists, energy, *refs):
    count = len(CHUNKS)
    products, own_terms = refs[:count], refs[count : 2 * count]
    total, energies = refs[2 * count : 2 * count + 2]
    refs = refs[2 * count + 2 :]
    returned, sums, slabs = refs[:count], refs[count : 2 * count], refs[2 * count : 3 * count]
    column, peer_send, peer_receive, level_send, level_receive = refs[3 * count :]
    me, level = lax.axis_index("orb"), lax.axis_index("grid")
    greet(me, level)
    spreads, exchanges = [], []
    for k in range(count):
        exchanges.append(
            Exchange(
                me, level,
                lambda a, k=k: products[k].at[pl.ds(a * CAP, CAP)],
                lambda a, k=k: returned[k].at[pl.ds(a * CAP, CAP)],
                peer_send.at[k], peer_receive.at[k],
            )
        )
        spreads.append(
            Spread(
                me, level,
                lambda other, k=k: sums[k].at[other],
                lambda other, k=k: slabs[k].at[other],
                level_send.at[k], level_receive.at[k],
            )
        )
    levels = Spread(
        me, level, lambda other: energy, lambda other: column.at[other],
        level_send.at[count], level_receive.at[count],
    )
    near = Exchange(
        me, level, lambda a: column, lambda a: energies.at[level, a],
        peer_send.at[count], peer_receive.at[count],
    )
    far = Spread(
        me, level, lambda other: energies.at[level], lambda other: energies.at[other],
        level_send.at[count + 1], level_receive.at[count + 1],
    )
    levels.start()
    for exchange in exchanges:
        exchange.start()
    column[level] = energy[...]
    asked, ahead = selectors(me, level, lists, mine)
    both = jnp.concatenate([asked, ahead], 0).T.astype(BF16)
    levels.wait_recv()
    near.start()
    for k, (at, width) in enumerate(CHUNKS):
        exchanges[k].wait_recv()
        planes = sums[k].reshape(EDGE, ORB_DEV, width)
        for start in range(0, EDGE, 8):
            rows = slice(start, start + 8)
            boxes = jnp.concatenate(
                [
                    returned[k][:, rows, :].reshape(256, width),
                    own_terms[k][:, rows, :].reshape(256, width),
                ],
                0,
            )
            out = jnp.dot(both, boxes, preferred_element_type=F32)
            planes[rows] = out.reshape(8, ORB_DEV, width).astype(BF16)
        spreads[k].start()
        if k == 0:
            near.wait_recv()
            far.start()
    for k, (at, width) in enumerate(CHUNKS):
        spreads[k].wait_recv()
        out = sums[k][level].astype(F32)
        for step in range(1, LEVELS):
            out = out + slabs[k][lax.rem(level + step, LEVELS)].astype(F32)
        total[:, :, at : at + width] = out
    far.wait_recv()
    for part in [levels, near, far] + spreads + exchanges:
        part.wait_send()


class TiledBoxes:
    def __init__(self, refs):
        self.refs = refs

    def at(self, slot, at, width):
        for ref, (start, size) in zip(self.refs, CHUNKS):
            if start <= at < start + size:
                return ref.at[slot, :, pl.ds(at - start, width)]

    def load(self, slot, at, width):
        return self.at(slot, at, width)[...].astype(F32)

    def store(self, slot, at, width, value):
        self.at(slot, at, width)[...] = value


def shift_tiles(pad, along_z, deltas, emit):
    dx, dy, dz = deltas
    start = LEFT + EDGE * dy + dz
    whole = lax.div(start, 128)
    part = start - whole * 128
    turn = lax.rem(128 - part, 128)
    lane = lax.broadcasted_iota(jnp.int32, (EDGE, 128), 1)
    from_here = lane < 128 - part
    rows = pl.ds(TOP + dx, EDGE)

    def turned(tile):
        return pltpu.roll(pad[whole + tile, rows, :], turn, 1)

    here = turned(0)
    for tile, (at, width) in enumerate(TILES):
        after = turned(tile + 1)
        out = jnp.where(from_here, here, after)
        z = along_z[:, at : at + 128] + dz
        inside = (z >= 0) & (z < EDGE)
        out = jnp.where(inside[None], out.reshape(EDGE // 8, 8, 128), 0.0).reshape(EDGE, 128)
        emit(at, width, out)
        here = after


def solve_kernel(place, mine, offset, *refs):
    count_of = len(CHUNKS)
    groups = [refs[n * count_of : (n + 1) * count_of] for n in range(2)]
    partners, phis = [TiledBoxes(group) for group in groups]
    sine_pair, plane, green, along_z = refs[2 * count_of : 2 * count_of + 4]
    refs = refs[2 * count_of + 4 :]
    groups = [refs[n * count_of : (n + 1) * count_of] for n in range(2)]
    returned, own_terms = [TiledBoxes(group) for group in groups]
    energies = refs[2 * count_of]
    refs = refs[2 * count_of + 1 :]
    live, places, pad, den, stack, forward, scaled, inverse, shifted, potential = refs
    me, level = place[0], place[1]
    for a in range(PEERS):
        places[a] = peer_of(me, level, a)

    def clear(at, _):
        energies[at] = 0.0
        return 0

    lax.fori_loop(0, 128, clear, 0)

    def place_of(slot):
        return places[lax.div(slot, CAP)] * CAP + lax.rem(slot, CAP)

    def compact(slot, count):
        alive = mine[place_of(slot)] >= 0

        @pl.when(alive)
        def _():
            live[count] = slot

        @pl.when(jnp.logical_not(alive))
        def _():
            for at, width in TILES:
                returned.store(slot, at, width, jnp.zeros((EDGE, width), BF16))
                own_terms.store(slot, at, width, jnp.zeros((EDGE, width), BF16))

        return count + alive.astype(jnp.int32)

    count = lax.fori_loop(0, SLOTS, compact, jnp.int32(0))
    pad[...] = jnp.zeros_like(pad)
    den[...] = jnp.zeros_like(den)

    def deltas_of(slot):
        at = place_of(slot)
        i = (me * ORB_DEV + mine[128 + at]) * 3
        j = (places[lax.div(slot, CAP)] * ORB_DEV + mine[at]) * 3
        return tuple(offset[i + axis] - offset[j + axis] for axis in range(3))

    def split(value):
        high = value.astype(BF16)
        return high, (value - high.astype(F32)).astype(BF16)

    def sine_product(cols):
        return jnp.dot(sine_pair[...], stack[:, cols], preferred_element_type=F32)

    def batch(index, _):
        base = index * BATCH
        pairs = lax.div(jnp.minimum(count - base, BATCH) + 1, 2)

        def before(pair, _):
            for side in range(2):
                position = base + pair * 2 + side
                rows = pl.ds(pl.multiple_of(pair * 80 + side * EDGE, 8), EDGE)

                @pl.when(position < count)
                def _():
                    slot = live[position]
                    for at, width in TILES:
                        pad[(LEFT + at) // 128, TOP : TOP + EDGE, :width] = partners.load(
                            slot, at, width
                        )

                    def emit(at, width, out):
                        shifted[rows, at : at + 128] = out
                        phi = phis.load(slot, at, width)
                        den[side * EDGE : (side + 1) * EDGE, at : at + width] = (
                            phi * out[:, :width]
                        )

                    shift_tiles(pad, along_z, deltas_of(slot), emit)

            for at, width in TILES:
                cols = slice(at, at + width)
                high, low = split(den[:, cols])
                stack[0:80, cols] = high
                stack[80:160, cols] = low
                stack[160:240, cols] = high
            rows = pl.ds(pl.multiple_of(pair * 80, 16), 80)
            for at, width in WIDE:
                cols = slice(at, at + width)
                forward[rows, cols] = sine_product(cols).astype(BF16)
            return 0

        lax.fori_loop(0, pairs, before, 0)

        def to_coeffs(step, _):
            cols = pl.ds(pl.multiple_of(step * 256, 256), 256)
            coeffs = jnp.dot(forward[...], plane[:, cols], preferred_element_type=F32)
            for pair in range(BATCH // 2):
                scaled[pair * 80 : pair * 80 + 80, cols] = (
                    green[:, cols] * coeffs[pair * 80 : pair * 80 + 80]
                ).astype(BF16)
            return 0

        lax.fori_loop(0, PADDED // 256, to_coeffs, 0)

        def to_inverse(step, _):
            cols = pl.ds(pl.multiple_of(step * 256, 256), 256)
            inverse[:, cols] = jnp.dot(
                scaled[:, :AREA], plane[:, cols], preferred_element_type=F32
            )
            return 0

        lax.fori_loop(0, PADDED // 256, to_inverse, 0)

        def after(pair, _):
            rows = pl.ds(pl.multiple_of(pair * 80, 16), 80)
            for at, width in TILES:
                cols = slice(at, at + width)
                high, low = split(inverse[rows, cols])
                stack[0:80, cols] = high
                stack[80:160, cols] = low
                stack[160:240, cols] = high
            for at, width in WIDE:
                cols = slice(at, at + width)
                potential[:, cols] = sine_product(cols)
            for side in range(2):
                position = base + pair * 2 + side
                half = pl.ds(pl.multiple_of(pair * 80 + side * EDGE, 8), EDGE)

                @pl.when(position < count)
                def _():
                    slot = live[position]
                    energy = jnp.zeros((EDGE, 128), F32)
                    for at, width in TILES:
                        cols = slice(at, at + width)
                        phi = phis.load(slot, at, width)
                        solved = potential[side * EDGE : (side + 1) * EDGE, cols]
                        term = solved * shifted[half, cols]
                        own_terms.store(slot, at, width, term.astype(BF16))
                        cell = term * phi
                        if width < 128:
                            cell = jnp.concatenate(
                                [cell, jnp.zeros((EDGE, 128 - width), F32)], 1
                            )
                        energy = energy + cell
                        pad[(LEFT + at) // 128, TOP : TOP + EDGE, :width] = (
                            (solved * phi).astype(BF16).astype(F32)
                        )
                    energies[place_of(slot)] = jnp.sum(energy) / (EDGE * EDGE * EDGE)

                    back = tuple(-delta for delta in deltas_of(slot))

                    def emit(at, width, out):
                        returned.store(slot, at, width, out[:, :width].astype(BF16))

                    shift_tiles(pad, along_z, back, emit)

            return 0

        lax.fori_loop(0, pairs, after, 0)
        return 0

    lax.fori_loop(0, lax.div(count + BATCH - 1, BATCH), batch, 0)


def gram_kernel(place, lists, energies, gram, half):
    orbitals = gram.shape[0]
    row = lax.broadcasted_iota(jnp.int32, (orbitals, 128), 0)
    slot = lax.broadcasted_iota(jnp.int32, (orbitals, 128), 1)
    owner_here = lax.div(row, ORB_DEV) == lax.div(slot, CAP)
    within = lax.rem(row, ORB_DEV)
    first_row = lax.broadcasted_iota(jnp.int32, (ORB_DEV, 128), 0)
    for a in range(PEERS):

        def owner(level, _):
            here = lists[level, a]
            energy = jnp.sum(energies[level, a], axis=0)
            second = (owner_here & (within == here[0:1])).astype(F32).astype(BF16)
            value = jnp.where(first_row == here[1:2], energy, 0.0)
            high = value.astype(BF16)
            rest = value - high.astype(F32)
            middle = rest.astype(BF16)
            low = (rest - middle.astype(F32)).astype(BF16)
            parts = jnp.concatenate([high, middle, low], 0)
            out = lax.dot_general(
                parts, second, (((1,), (1,)), ((), ())), preferred_element_type=F32
            )
            start = peer_of(place[0], level, a) * ORB_DEV
            rows = pl.ds(pl.multiple_of(start, ORB_DEV), ORB_DEV)
            half[rows, :] = out[0:32] + out[32:64] + out[64:96]
            return 0

        lax.fori_loop(0, LEVELS, owner, 0)
    for y in range(0, orbitals, 128):
        for x in range(0, orbitals, 128):
            gram[y : y + 128, x : x + 128] = (
                half[y : y + 128, x : x + 128] + half[x : x + 128, y : y + 128].T
            )


def params(mebibytes, **more):
    return pltpu.CompilerParams(vmem_limit_bytes=mebibytes * 2**20, **more)


BOXES = [jax.ShapeDtypeStruct((SLOTS, EDGE, width), BF16) for _, width in CHUNKS]
COUNT = len(CHUNKS)


def semaphores(extra):
    return [
        pltpu.SemaphoreType.DMA((COUNT + 1, PEERS)),
        pltpu.SemaphoreType.DMA((COUNT + 1, PEERS)),
        pltpu.SemaphoreType.DMA((COUNT + extra, LEVELS)),
        pltpu.SemaphoreType.DMA((COUNT + extra, LEVELS)),
    ]


def fetch(mine, own):
    slab = own.shape[0]
    outs = pl.pallas_call(
        fetch_kernel,
        out_shape=(*BOXES, *BOXES, jax.ShapeDtypeStruct((LEVELS, PEERS, 2, 128), jnp.int32)),
        in_specs=[VMEM] * 2,
        out_specs=(VMEM,) * (2 * COUNT + 1),
        scratch_shapes=[
            *[pltpu.VMEM((LEVELS, slab, ORB_DEV, width), BF16) for _, width in CHUNKS],
            *[pltpu.VMEM((SLOTS, EDGE, width), BF16) for _, width in CHUNKS],
            *semaphores(1),
        ],
        compiler_params=params(56, collective_id=1, has_side_effects=True),
        name="fetch",
    )(mine, own)
    return outs[:COUNT], outs[COUNT : 2 * COUNT], outs[2 * COUNT]


def solve(place, mine, offset, partners, phis):
    constants = [jnp.asarray(table) for table in tables()]
    outs = pl.pallas_call(
        solve_kernel,
        out_shape=(*BOXES, *BOXES, jax.ShapeDtypeStruct((128,), F32)),
        in_specs=[SMEM] * 3 + [VMEM] * (2 * COUNT + 4),
        out_specs=(VMEM,) * (2 * COUNT) + (SMEM,),
        scratch_shapes=[
            pltpu.SMEM((SLOTS + 8,), jnp.int32),
            pltpu.SMEM((PEERS,), jnp.int32),
            pltpu.VMEM((27, 88, 128), F32),
            pltpu.VMEM((80, 1664), F32),
            pltpu.VMEM((240, AREA), BF16),
            pltpu.VMEM((BATCH * EDGE, AREA), BF16),
            pltpu.VMEM((BATCH * EDGE, PADDED), BF16),
            pltpu.VMEM((BATCH * EDGE, PADDED), F32),
            pltpu.VMEM((BATCH * EDGE, 1664), F32),
            pltpu.VMEM((80, AREA), F32),
        ],
        compiler_params=params(58),
        name="solve",
    )(place, mine, offset, *partners, *phis, *constants)
    return outs[:COUNT], outs[COUNT : 2 * COUNT], outs[2 * COUNT]


def give_back(mine, lists, energy, products, own_terms, slab):
    return pl.pallas_call(
        give_back_kernel,
        out_shape=(
            jax.ShapeDtypeStruct((slab, ORB_DEV, AREA), F32),
            jax.ShapeDtypeStruct((LEVELS, PEERS, LEVELS, 1, 128), F32),
        ),
        in_specs=[VMEM] * (3 + 2 * COUNT),
        out_specs=(VMEM,) * 2,
        scratch_shapes=[
            *[pltpu.VMEM((SLOTS, EDGE, width), BF16) for _, width in CHUNKS],
            *[pltpu.VMEM((LEVELS, slab, ORB_DEV, width), BF16) for _, width in CHUNKS],
            *[pltpu.VMEM((LEVELS, slab, ORB_DEV, width), BF16) for _, width in CHUNKS],
            pltpu.VMEM((LEVELS, 1, 128), F32),
            *semaphores(2),
        ],
        compiler_params=params(56, collective_id=2, has_side_effects=True),
        name="give_back",
    )(mine, lists, energy, *products, *own_terms)


def gram_of(place, lists, energies, orbitals):
    return pl.pallas_call(
        gram_kernel,
        out_shape=jax.ShapeDtypeStruct((orbitals, orbitals), F32),
        in_specs=[SMEM, VMEM, VMEM],
        out_specs=VMEM,
        scratch_shapes=[pltpu.VMEM((orbitals, orbitals), F32)],
        compiler_params=params(32),
        name="gram",
    )(place, lists, energies)


def on_device(orbitals, box_offset, partner_slot, first_slot):
    place = jnp.stack([lax.axis_index("orb"), lax.axis_index("grid")]).astype(jnp.int32)
    mine = jnp.concatenate([partner_slot, first_slot], 0).reshape(2, -1)
    partners, phis, lists = fetch(mine, orbitals.transpose(1, 0, 2))
    products, own_terms, energy = solve(
        place, mine.reshape(-1), box_offset.reshape(-1), partners, phis
    )
    terms, energies = give_back(
        mine, lists, energy.reshape(1, -1), products, own_terms, orbitals.shape[1]
    )
    gram = gram_of(place, lists, energies, box_offset.shape[0])
    return (terms.transpose(1, 0, 2), gram)


def solution(mesh):
    placed = (P("orb", "grid", None), P(), P("orb", None, None), P("orb", None, None))
    return jax.shard_map(
        on_device,
        mesh=mesh,
        in_specs=placed,
        out_specs=(P("orb", "grid", None), P()),
        check_vma=False,
    )
```

```python
import functools
import math

import jax
import jax.numpy as jnp
import ml_dtypes
import numpy as np
from jax import lax
from jax.experimental import pallas as pl
from jax.experimental.pallas import tpu as pltpu
from jax.sharding import PartitionSpec as P

BF16 = jnp.bfloat16
F32 = jnp.float32
VMEM = pl.BlockSpec(memory_space=pltpu.VMEM)
SMEM = pl.BlockSpec(memory_space=pltpu.SMEM)
EDGE = 40
AREA = 1600
ORB_DEV = 32
CAP = 4
SLOTS = 32
BATCH = 8
PADDED = 1792
STEP = 896
TOP = 24
LEFT = 896
TILES = [(at, min(128, AREA - at)) for at in range(0, AREA, 128)]
CHUNKS = [(0, 256), (256, 256), (512, 384), (896, 384), (1280, 320)]
COUNT = len(CHUNKS)
PEERS = 8
LEVELS = 4
MESH = pl.DeviceIdType.MESH
WIDE = [(at, min(256, AREA - at)) for at in range(0, AREA, 256)]


@functools.cache
def tables():
    number = np.arange(EDGE, dtype=np.float64) + 1.0
    sine = np.sqrt(2.0 / (EDGE + 1.0)) * np.sin(
        math.pi * number[:, None] * number[None, :] / (EDGE + 1.0)
    )
    sine32 = sine.astype(np.float32)
    plane = (sine32[:, None, :, None] * sine32[None, :, None, :]).reshape(AREA, AREA)
    plane = np.pad(plane, ((0, 0), (0, PADDED - AREA))).astype(ml_dtypes.bfloat16)
    eigen = 2.0 - 2.0 * np.cos(math.pi * number / (EDGE + 1.0))
    green = 1.0 / (eigen[:, None, None] + eigen[None, :, None] + eigen[None, None, :])
    green = np.pad(green.reshape(EDGE, AREA), ((0, 0), (0, PADDED - AREA)))
    green = np.tile(green.astype(np.float32), (2, 1))
    high = sine32.astype(ml_dtypes.bfloat16)
    low = (sine32 - high.astype(np.float32)).astype(ml_dtypes.bfloat16)
    two = np.eye(2, dtype=np.float32)
    pair_high = np.kron(two, high.astype(np.float32))
    pair_low = np.kron(two, low.astype(np.float32))
    sine_pair = np.concatenate([pair_high, pair_high, pair_low], 1).astype(ml_dtypes.bfloat16)
    along_z = np.tile(np.arange(1664, dtype=np.int32) % EDGE, (8, 1))
    return sine_pair, plane, green, along_z


def rem(value, by):
    return value % by if isinstance(value, int) else lax.rem(value, jnp.int32(by))


def div(value, by):
    return value // by if isinstance(value, int) else lax.div(value, jnp.int32(by))


def owner_at(me, level, r, sign):
    kind = level + div(r, 4) * (3 - 2 * level)
    x = rem(div(me, 2) + 8 + sign * (2 * rem(r, 2) + rem(kind, 2)), 4)
    y = rem(div(me, 8) + 8 + sign * (2 * rem(div(r, 2), 2) + div(kind, 2)), 4)
    return y * 8 + x * 2 + rem(me + div(r, 4), 2)


def peer_of(me, level, r):
    return owner_at(me, level, r, 1)


def asker_of(me, level, r):
    return owner_at(me, level, r, -1)


def selector(index_of):
    column = lax.broadcasted_iota(jnp.int32, (8, 256), 1)
    row = lax.broadcasted_iota(jnp.int32, (8, 256), 0)
    offset = column - row * ORB_DEV
    blocks = []
    for slot in range(SLOTS):
        index = index_of(slot // CAP, slot % CAP)
        index = jnp.where(index < 0, 100000, index)
        blocks.append((offset == index).astype(F32))
    return jnp.concatenate(blocks, 0)


def entry(row, at):
    lane = lax.broadcasted_iota(jnp.int32, (1, 128), 1)
    return jnp.sum(jnp.where(lane == at, row, 0), axis=1, keepdims=True)


def selectors(me, level, lists, mine):
    asked = selector(lambda r, c: entry(lists[level, r, 0:1, :], me * CAP + c))
    ahead = selector(lambda r, c: entry(mine[1:2, :], peer_of(me, level, r) * CAP + c))
    return asked, ahead


def greet(me, level):
    barrier = pltpu.get_barrier_semaphore()
    for a in range(1, PEERS):
        pl.semaphore_signal(
            barrier, inc=1, device_id=(peer_of(me, level, a), level), device_id_type=MESH
        )
    for step in range(1, LEVELS):
        pl.semaphore_signal(
            barrier, inc=1, device_id=(me, lax.rem(level + step, LEVELS)), device_id_type=MESH
        )

    @pl.when(level != 0)
    def _():
        pl.semaphore_signal(
            barrier, inc=1, device_id=(peer_of(me, level, 0), level), device_id_type=MESH
        )
        pl.semaphore_wait(barrier, PEERS + LEVELS - 1)

    @pl.when(level == 0)
    def _():
        pl.semaphore_wait(barrier, PEERS + LEVELS - 2)


class Exchange:
    def __init__(self, level, r, owner, source, target, send, receive):
        self.level, self.r = level, r
        self.remote = pltpu.make_async_remote_copy(
            source, target, send, receive, device_id=(owner, level), device_id_type=MESH
        )
        self.local = pltpu.make_async_copy(source, target, send) if r == 0 else None

    def both(self, remote, local):
        if self.r != 0:
            remote()
            return

        pl.when(self.level != 0)(remote)
        if local is not None:
            pl.when(self.level == 0)(local)

    def start(self):
        self.both(
            lambda: self.remote.start(), lambda: self.local.start()
        )

    def wait_recv(self):
        self.both(lambda: self.remote.wait_recv(), lambda: self.local.wait())

    def wait_send(self):
        self.both(lambda: self.remote.wait_send(), None)


class Spread:
    def __init__(self, me, level, source, target, send, receive):
        self.copies = []
        for step in range(1, LEVELS):
            other = lax.rem(level + step, LEVELS)
            self.copies.append(
                pltpu.make_async_remote_copy(
                    source(other),
                    target(level),
                    send.at[step],
                    receive.at[step],
                    device_id=(me, other),
                    device_id_type=MESH,
                )
            )
        self.arrivals = []
        for step in range(1, LEVELS):
            other = lax.rem(level + LEVELS - step, LEVELS)
            self.arrivals.append(
                pltpu.make_async_remote_copy(
                    source(other),
                    target(other),
                    send.at[step],
                    receive.at[step],
                    device_id=(me, other),
                    device_id_type=MESH,
                )
            )

    def start(self):
        for copy in self.copies:
            copy.start()

    def wait_recv(self):
        for copy in self.arrivals:
            copy.wait_recv()

    def wait_send(self):
        for copy in self.copies:
            copy.wait_send()


class TiledBoxes:
    def __init__(self, refs):
        self.refs = refs

    def at(self, slot, at, width):
        for ref, (start, size) in zip(self.refs, CHUNKS):
            if start <= at < start + size:
                return ref.at[slot, :, pl.ds(at - start, width)]

    def load(self, slot, at, width):
        return self.at(slot, at, width)[...].astype(F32)

    def store(self, slot, at, width, value):
        self.at(slot, at, width)[...] = value


def shift_tiles(pad, along_z, deltas, emit):
    dx, dy, dz = deltas
    start = LEFT + EDGE * dy + dz
    whole = lax.div(start, 128)
    part = start - whole * 128
    turn = lax.rem(128 - part, 128)
    lane = lax.broadcasted_iota(jnp.int32, (EDGE, 128), 1)
    from_here = lane < 128 - part
    rows = pl.ds(TOP + dx, EDGE)

    def turned(tile):
        return pltpu.roll(pad[whole + tile, rows, :], turn, 1)

    here = turned(0)
    for tile, (at, width) in enumerate(TILES):
        after = turned(tile + 1)
        out = jnp.where(from_here, here, after)
        z = along_z[:, at : at + 128] + dz
        inside = (z >= 0) & (z < EDGE)
        out = jnp.where(inside[None], out.reshape(EDGE // 8, 8, 128), 0.0).reshape(EDGE, 128)
        emit(at, width, out)
        here = after


def solve_group(me, level, group, mine, offset, partners, phis, tables, scratch, energy):
    partners, phis, returned, own_terms = [TiledBoxes(boxes) for boxes in (*partners, *phis)]
    sine_pair, plane, green, along_z = tables
    pad, den, stack, forward, scaled, inverse, shifted, potential = scratch

    def place_of(slot):
        return peer_of(me, level, div(slot, CAP)) * CAP + rem(slot, CAP)

    def deltas_of(slot):
        at = place_of(slot)
        i = (me * ORB_DEV + jnp.maximum(mine[128 + at], 0)) * 3
        j = (peer_of(me, level, div(slot, CAP)) * ORB_DEV + jnp.maximum(mine[at], 0)) * 3
        return tuple(offset[i + axis] - offset[j + axis] for axis in range(3))

    def split(value):
        high = value.astype(BF16)
        return high, (value - high.astype(F32)).astype(BF16)

    def sine_product(cols):
        return jnp.dot(sine_pair[...], stack[:, cols], preferred_element_type=F32)

    def before(pair, _):
        for side in range(2):
            slot = group * BATCH + pair * 2 + side
            rows = pl.ds(pl.multiple_of(pair * 80 + side * EDGE, 8), EDGE)
            for at, width in TILES:
                pad[(LEFT + at) // 128, TOP : TOP + EDGE, :width] = partners.load(
                    slot, at, width
                )

            def emit(at, width, out):
                shifted[rows, at : at + 128] = out
                phi = phis.load(slot, at, width)
                den[side * EDGE : (side + 1) * EDGE, at : at + width] = phi * out[:, :width]

            shift_tiles(pad, along_z, deltas_of(slot), emit)
        for at, width in TILES:
            cols = slice(at, at + width)
            high, low = split(den[:, cols])
            stack[0:80, cols] = high
            stack[80:160, cols] = low
            stack[160:240, cols] = high
        rows = pl.ds(pl.multiple_of(pair * 80, 16), 80)
        for at, width in WIDE:
            cols = slice(at, at + width)
            forward[rows, cols] = sine_product(cols).astype(BF16)
        return 0

    lax.fori_loop(0, BATCH // 2, before, 0)

    def to_coeffs(step, _):
        cols = pl.ds(pl.multiple_of(step * STEP, 128), STEP)
        coeffs = jnp.dot(forward[...], plane[:, cols], preferred_element_type=F32)
        for pair in range(BATCH // 2):
            scaled[pair * 80 : pair * 80 + 80, cols] = (
                green[:, cols] * coeffs[pair * 80 : pair * 80 + 80]
            ).astype(BF16)
        return 0

    lax.fori_loop(0, PADDED // STEP, to_coeffs, 0)

    def to_inverse(step, _):
        cols = pl.ds(pl.multiple_of(step * STEP, 128), STEP)
        inverse[:, cols] = jnp.dot(
            scaled[:, :AREA], plane[:, cols], preferred_element_type=F32
        )
        return 0

    lax.fori_loop(0, PADDED // STEP, to_inverse, 0)

    def after(pair, _):
        rows = pl.ds(pl.multiple_of(pair * 80, 16), 80)
        for at, width in TILES:
            cols = slice(at, at + width)
            high, low = split(inverse[rows, cols])
            stack[0:80, cols] = high
            stack[80:160, cols] = low
            stack[160:240, cols] = high
        for at, width in WIDE:
            cols = slice(at, at + width)
            potential[:, cols] = sine_product(cols)
        for side in range(2):
            slot = group * BATCH + pair * 2 + side
            half = pl.ds(pl.multiple_of(pair * 80 + side * EDGE, 8), EDGE)
            cells = jnp.zeros((EDGE, 128), F32)
            for at, width in TILES:
                cols = slice(at, at + width)
                phi = phis.load(slot, at, width)
                solved = potential[side * EDGE : (side + 1) * EDGE, cols]
                term = solved * shifted[half, cols]
                own_terms.store(slot, at, width, term.astype(BF16))
                cell = term * phi
                if width < 128:
                    cell = jnp.concatenate([cell, jnp.zeros((EDGE, 128 - width), F32)], 1)
                cells = cells + cell
                pad[(LEFT + at) // 128, TOP : TOP + EDGE, :width] = (
                    (solved * phi).astype(BF16).astype(F32)
                )
            value = jnp.sum(jnp.sum(cells, axis=0, keepdims=True), axis=1, keepdims=True)
            lane = lax.broadcasted_iota(jnp.int32, (1, 128), 1)
            energy[...] += jnp.where(
                lane == place_of(slot), value / (EDGE * EDGE * EDGE), 0.0
            )
            back = tuple(-delta for delta in deltas_of(slot))

            def emit(at, width, out):
                returned.store(slot, at, width, out[:, :width].astype(BF16))

            shift_tiles(pad, along_z, back, emit)
        return 0

    lax.fori_loop(0, BATCH // 2, after, 0)


def add_gram(me, lists, energies, gram, half):
    orbitals = gram.shape[0]
    row = lax.broadcasted_iota(jnp.int32, (orbitals, 128), 0)
    slot = lax.broadcasted_iota(jnp.int32, (orbitals, 128), 1)
    owner_here = lax.div(row, ORB_DEV) == lax.div(slot, CAP)
    within = lax.rem(row, ORB_DEV)
    first_row = lax.broadcasted_iota(jnp.int32, (ORB_DEV, 128), 0)

    def owner(index, _):
        level, r = div(index, PEERS), rem(index, PEERS)
        here = lists[level, r]
        energy = jnp.sum(energies[level, r], axis=0)
        second = (owner_here & (within == here[0:1])).astype(F32).astype(BF16)
        value = jnp.where(first_row == here[1:2], energy, 0.0)
        high = value.astype(BF16)
        rest = value - high.astype(F32)
        middle = rest.astype(BF16)
        low = (rest - middle.astype(F32)).astype(BF16)
        parts = jnp.concatenate([high, middle, low], 0)
        out = lax.dot_general(
            parts, second, (((1,), (1,)), ((), ())), preferred_element_type=F32
        )
        rows = pl.ds(pl.multiple_of(asker_of(me, level, r) * ORB_DEV, ORB_DEV), ORB_DEV)
        half[rows, :] = out[0:32] + out[32:64] + out[64:96]
        return 0

    lax.fori_loop(0, LEVELS * PEERS, owner, 0)
    for y in range(0, orbitals, 128):
        for x in range(0, orbitals, 128):
            gram[y : y + 128, x : x + 128] = (
                half[y : y + 128, x : x + 128] + half[x : x + 128, y : y + 128].T
            )


def exchange_kernel(
    mine_scalars, offset, mine, own, sine_pair, plane_source, green, along_z,
    total, gram, *refs,
):
    count = COUNT
    gathered, picked, partners, phis, returned, slabs = [
        refs[n * count : (n + 1) * count] for n in range(6)
    ]
    sums, products, own_terms = gathered, picked, partners
    refs = refs[6 * count :]
    lists, energy, column, energies, half, plane = refs[:6]
    scratch = refs[6:14]
    list_send, list_receive, out_send, out_receive, back_send, back_receive = refs[14:20]
    value_send, value_receive, level_send, level_receive, plane_sem = refs[20:]
    me, level = lax.axis_index("orb"), lax.axis_index("grid")

    out, back, near, values = [], [], [], []
    for r in range(PEERS):
        block = pl.ds(r * CAP, CAP)
        asker, peer = asker_of(me, level, r), peer_of(me, level, r)
        out.append([
            Exchange(level, r, asker, picked[k].at[block], partners[k].at[block],
                     out_send.at[k, r], out_receive.at[k, r])
            for k in range(count)
        ])
        back.append([
            Exchange(level, r, peer, products[k].at[block], returned[k].at[block],
                     back_send.at[k, r], back_receive.at[k, r])
            for k in range(count)
        ])
        near.append(
            Exchange(level, r, peer, mine, lists.at[level, r],
                     list_send.at[r], list_receive.at[r])
        )
        values.append(
            Exchange(level, r, peer, column, energies.at[level, r],
                     value_send.at[r], value_receive.at[r])
        )
    gathers, scatters = [], []
    for k, (at, width) in enumerate(CHUNKS):
        gathers.append(
            Spread(
                me, level,
                lambda other, at=at, width=width: own.at[:, :, pl.ds(at, width)],
                lambda other, k=k: gathered[k].at[other],
                level_send.at[k], level_receive.at[k],
            )
        )
        scatters.append(
            Spread(
                me, level,
                lambda other, k=k: sums[k].at[other],
                lambda other, k=k: slabs[k].at[other],
                level_send.at[count + k], level_receive.at[count + k],
            )
        )
    far = Spread(
        me, level, lambda other: lists.at[level], lambda other: lists.at[other],
        level_send.at[2 * count], level_receive.at[2 * count],
    )
    levels = Spread(
        me, level, lambda other: energy, lambda other: column.at[other],
        level_send.at[2 * count + 1], level_receive.at[2 * count + 1],
    )
    far_values = Spread(
        me, level, lambda other: energies.at[level], lambda other: energies.at[other],
        level_send.at[2 * count + 2], level_receive.at[2 * count + 2],
    )
    load_plane = pltpu.make_async_copy(plane_source, plane, plane_sem)

    load_plane.start()
    greet(me, level)
    for copy in near:
        copy.start()
    for gather in gathers:
        gather.start()
    for k, (at, width) in enumerate(CHUNKS):
        gathered[k][level] = own[:, :, at : at + width]
    energy[...] = jnp.zeros_like(energy)
    scratch[0][...] = jnp.zeros_like(scratch[0])
    for copy in near:
        copy.wait_recv()
    far.start()
    asked, ahead = selectors(me, level, lists, mine)
    both = jnp.concatenate([asked, ahead], 0).astype(BF16)

    def send_out(rs, k):
        if 0 <= k < count:
            for r in rs:
                out[r][k].start()

    for k, (at, width) in enumerate(CHUNKS):
        gathers[k].wait_recv()
        planes = gathered[k].reshape(EDGE, ORB_DEV, width)
        for start in range(0, EDGE, 8):
            source = planes[start : start + 8].reshape(256, width)
            boxes = jnp.dot(both, source, preferred_element_type=F32).astype(BF16)
            boxes = boxes.reshape(2 * SLOTS, 8, width)
            picked[k][:, start : start + 8, :] = boxes[:SLOTS]
            phis[k][:, start : start + 8, :] = boxes[SLOTS:]
        send_out(range(4), k)
        send_out(range(4, PEERS), k - 1)
    send_out(range(4, PEERS), count - 1)
    far.wait_recv()
    load_plane.wait()

    for group in range(LEVELS):
        rs = (2 * group, 2 * group + 1)
        for r in rs:
            for k in range(count):
                out[r][k].wait_recv()
                out[r][k].wait_send()
        solve_group(
            me, level, group, mine_scalars, offset,
            (partners, phis), (products, own_terms),
            (sine_pair, plane, green, along_z), scratch, energy,
        )
        for k in range(count):
            if group < 2 or k < 2:
                for r in rs:
                    back[r][k].start()
    levels.start()
    column[level] = energy[...]
    back_select = jnp.concatenate([asked, ahead], 0).T.astype(BF16)
    levels.wait_recv()
    for copy in values:
        copy.start()
    for k, (at, width) in enumerate(CHUNKS):
        for r in range(PEERS):
            back[r][k].wait_recv()
        if k + 2 < count:
            for r in range(4, PEERS):
                back[r][k + 2].start()
        planes = sums[k].reshape(EDGE, ORB_DEV, width)
        for start in range(0, EDGE, 8):
            rows = slice(start, start + 8)
            boxes = jnp.concatenate(
                [
                    returned[k][:, rows, :].reshape(256, width),
                    own_terms[k][:, rows, :].reshape(256, width),
                ],
                0,
            )
            slab = jnp.dot(back_select, boxes, preferred_element_type=F32)
            planes[rows] = slab.reshape(8, ORB_DEV, width).astype(BF16)
        scatters[k].start()
        if k == 0:
            for copy in values:
                copy.wait_recv()
            far_values.start()
    far_values.wait_recv()
    add_gram(me, lists, energies, gram, half)
    for k, (at, width) in enumerate(CHUNKS):
        scatters[k].wait_recv()
        slab = sums[k][level].astype(F32)
        for step in range(1, LEVELS):
            slab = slab + slabs[k][lax.rem(level + step, LEVELS)].astype(F32)
        total[:, :, at : at + width] = slab
    for copy in near + values + [copy for copies in back for copy in copies]:
        copy.wait_send()
    for spread in [far, levels, far_values] + gathers + scatters:
        spread.wait_send()


def params(mebibytes, **more):
    return pltpu.CompilerParams(vmem_limit_bytes=mebibytes * 2**20, **more)


def exchange(mine, offset, own):
    slab, orbitals = own.shape[0], offset.shape[0] // 3
    constants = [jnp.asarray(table) for table in tables()]
    boxes = [pltpu.VMEM((SLOTS, EDGE, width), BF16) for _, width in CHUNKS]
    slabs = [pltpu.VMEM((LEVELS, slab, ORB_DEV, width), BF16) for _, width in CHUNKS]
    any_place = pl.BlockSpec(memory_space=pl.ANY)
    dma = pltpu.SemaphoreType.DMA
    return pl.pallas_call(
        exchange_kernel,
        out_shape=(
            jax.ShapeDtypeStruct((slab, ORB_DEV, AREA), F32),
            jax.ShapeDtypeStruct((orbitals, orbitals), F32),
        ),
        in_specs=[SMEM, SMEM, VMEM, VMEM, VMEM, any_place, VMEM, VMEM],
        out_specs=(VMEM,) * 2,
        scratch_shapes=[
            *slabs, *boxes, *boxes, *boxes, *boxes, *slabs,
            pltpu.VMEM((LEVELS, PEERS, 2, 128), jnp.int32),
            pltpu.VMEM((1, 128), F32),
            pltpu.VMEM((LEVELS, 1, 128), F32),
            pltpu.VMEM((LEVELS, PEERS, LEVELS, 1, 128), F32),
            pltpu.VMEM((orbitals, orbitals), F32),
            pltpu.VMEM((AREA, PADDED), BF16),
            pltpu.VMEM((27, 88, 128), F32),
            pltpu.VMEM((80, 1664), F32),
            pltpu.VMEM((240, AREA), BF16),
            pltpu.VMEM((BATCH * EDGE, AREA), BF16),
            pltpu.VMEM((BATCH * EDGE, PADDED), BF16),
            pltpu.VMEM((BATCH * EDGE, PADDED), F32),
            pltpu.VMEM((BATCH * EDGE, 1664), F32),
            pltpu.VMEM((80, AREA), F32),
            dma((PEERS,)), dma((PEERS,)),
            dma((COUNT, PEERS)), dma((COUNT, PEERS)),
            dma((COUNT, PEERS)), dma((COUNT, PEERS)),
            dma((PEERS,)), dma((PEERS,)),
            dma((2 * COUNT + 3, LEVELS)), dma((2 * COUNT + 3, LEVELS)),
            dma(()),
        ],
        compiler_params=params(62, collective_id=1, has_side_effects=True),
        name="exchange",
    )(mine.reshape(-1), offset, mine, own, *constants)


def on_device(orbitals, box_offset, partner_slot, first_slot):
    mine = jnp.concatenate([partner_slot, first_slot], 0).reshape(2, -1)
    terms, gram = exchange(mine, box_offset.reshape(-1), orbitals.transpose(1, 0, 2))
    return (terms.transpose(1, 0, 2), gram)


def solution(mesh):
    placed = (P("orb", "grid", None), P(), P("orb", None, None), P("orb", None, None))
    return jax.shard_map(
        on_device,
        mesh=mesh,
        in_specs=placed,
        out_specs=(P("orb", "grid", None), P()),
        check_vma=False,
    )
```

```python
import functools
import math

import jax
import jax.numpy as jnp
import ml_dtypes
import numpy as np
from jax import lax
from jax.experimental import pallas as pl
from jax.experimental.pallas import tpu as pltpu
from jax.sharding import PartitionSpec as P

BF16 = jnp.bfloat16
F32 = jnp.float32
VMEM = pl.BlockSpec(memory_space=pltpu.VMEM)
SMEM = pl.BlockSpec(memory_space=pltpu.SMEM)
EDGE = 40
AREA = 1600
ORB_DEV = 32
CAP = 4
SLOTS = 32
BATCH = 8
PADDED = 1792
STEP = 896
AHEAD = 2
LAGS = (0,0,1,2)
AT_ONCE = (5,5,3,3)
TOP = 24
LEFT = 896
TILES = [(at, min(128, AREA - at)) for at in range(0, AREA, 128)]
WIDTHS = (256, 256, 384, 384, 320)
CHUNKS = [(sum(WIDTHS[:k]), width) for k, width in enumerate(WIDTHS)]
COUNT = len(CHUNKS)
PEERS = 8
LEVELS = 4
MESH = pl.DeviceIdType.MESH
WIDE = [(at, min(256, AREA - at)) for at in range(0, AREA, 256)]


@functools.cache
def tables():
    number = np.arange(EDGE, dtype=np.float64) + 1.0
    sine = np.sqrt(2.0 / (EDGE + 1.0)) * np.sin(
        math.pi * number[:, None] * number[None, :] / (EDGE + 1.0)
    )
    sine32 = sine.astype(np.float32)
    plane = (sine32[:, None, :, None] * sine32[None, :, None, :]).reshape(AREA, AREA)
    plane = np.pad(plane, ((0, 0), (0, PADDED - AREA))).astype(ml_dtypes.bfloat16)
    eigen = 2.0 - 2.0 * np.cos(math.pi * number / (EDGE + 1.0))
    green = 1.0 / (eigen[:, None, None] + eigen[None, :, None] + eigen[None, None, :])
    green = np.pad(green.reshape(EDGE, AREA), ((0, 0), (0, PADDED - AREA)))
    green = np.tile(green.astype(np.float32), (2, 1))
    high = sine32.astype(ml_dtypes.bfloat16)
    low = (sine32 - high.astype(np.float32)).astype(ml_dtypes.bfloat16)
    two = np.eye(2, dtype=np.float32)
    pair_high = np.kron(two, high.astype(np.float32))
    pair_low = np.kron(two, low.astype(np.float32))
    sine_pair = np.concatenate([pair_high, pair_high, pair_low], 1).astype(ml_dtypes.bfloat16)
    along_z = np.tile(np.arange(1664, dtype=np.int32) % EDGE, (8, 1))
    return sine_pair, plane, green, along_z


def rem(value, by):
    return value % by if isinstance(value, int) else lax.rem(value, jnp.int32(by))


def div(value, by):
    return value // by if isinstance(value, int) else lax.div(value, jnp.int32(by))


def owner_at(me, level, r, sign):
    kind = level + div(r, 4) * (3 - 2 * level)
    x = rem(div(me, 2) + 8 + sign * (2 * rem(r, 2) + rem(kind, 2)), 4)
    y = rem(div(me, 8) + 8 + sign * (2 * rem(div(r, 2), 2) + div(kind, 2)), 4)
    return y * 8 + x * 2 + rem(me + div(r, 4), 2)


def peer_of(me, level, r):
    return owner_at(me, level, r, 1)


def asker_of(me, level, r):
    return owner_at(me, level, r, -1)


def selector(index_of):
    column = lax.broadcasted_iota(jnp.int32, (8, 256), 1)
    row = lax.broadcasted_iota(jnp.int32, (8, 256), 0)
    offset = column - row * ORB_DEV
    blocks = []
    for slot in range(SLOTS):
        index = index_of(slot // CAP, slot % CAP)
        index = jnp.where(index < 0, 100000, index)
        blocks.append((offset == index).astype(F32))
    return jnp.concatenate(blocks, 0)


def entry(row, at):
    lane = lax.broadcasted_iota(jnp.int32, (1, 128), 1)
    return jnp.sum(jnp.where(lane == at, row, 0), axis=1, keepdims=True)


def selectors(me, level, lists, mine):
    asked = selector(lambda r, c: entry(lists[level, r, 0:1, :], me * CAP + c))
    ahead = selector(lambda r, c: entry(mine[1:2, :], peer_of(me, level, r) * CAP + c))
    return asked, ahead


def greet(me, level):
    barrier = pltpu.get_barrier_semaphore()
    for a in range(1, PEERS):
        pl.semaphore_signal(
            barrier, inc=1, device_id=(peer_of(me, level, a), level), device_id_type=MESH
        )
    for step in range(1, LEVELS):
        pl.semaphore_signal(
            barrier, inc=1, device_id=(me, lax.rem(level + step, LEVELS)), device_id_type=MESH
        )

    @pl.when(level != 0)
    def _():
        pl.semaphore_signal(
            barrier, inc=1, device_id=(peer_of(me, level, 0), level), device_id_type=MESH
        )
        pl.semaphore_wait(barrier, PEERS + LEVELS - 1)

    @pl.when(level == 0)
    def _():
        pl.semaphore_wait(barrier, PEERS + LEVELS - 2)


class Exchange:
    def __init__(self, level, r, owner, source, target, send, receive):
        self.level, self.r = level, r
        self.remote = pltpu.make_async_remote_copy(
            source, target, send, receive, device_id=(owner, level), device_id_type=MESH
        )
        self.local = pltpu.make_async_copy(source, target, send) if r == 0 else None

    def both(self, remote, local):
        if self.r != 0:
            remote()
            return

        pl.when(self.level != 0)(remote)
        if local is not None:
            pl.when(self.level == 0)(local)

    def start(self):
        self.both(
            lambda: self.remote.start(), lambda: self.local.start()
        )

    def wait_recv(self):
        self.both(lambda: self.remote.wait_recv(), lambda: self.local.wait())

    def wait_send(self):
        self.both(lambda: self.remote.wait_send(), None)


def hop(me, level, step, source, target, send, receive):
    return pltpu.make_async_remote_copy(
        source, target, send, receive,
        device_id=(me, lax.rem(level + step, LEVELS)), device_id_type=MESH,
    )


class RingGather:
    def __init__(self, me, level, own, gathered, send, receive):
        half = own.shape[0] // 2
        low, high = pl.ds(0, half), pl.ds(half, half)
        below, above = lax.rem(level + 3, LEVELS), lax.rem(level + 1, LEVELS)
        opposite = lax.rem(level + 2, LEVELS)

        def make(step, source, target, n):
            return hop(me, level, step, source, target, send.at[n], receive.at[n])

        self.near = [
            make(1, own, gathered.at[level], 0),
            make(3, own, gathered.at[level], 1),
        ]
        self.near_in = [
            make(1, own, gathered.at[below], 0),
            make(3, own, gathered.at[above], 1),
        ]
        self.far = [
            make(1, gathered.at[below, low], gathered.at[below, low], 2),
            make(3, gathered.at[above, high], gathered.at[above, high], 3),
        ]
        self.far_in = [
            make(1, gathered.at[below, low], gathered.at[opposite, low], 2),
            make(3, gathered.at[above, high], gathered.at[opposite, high], 3),
        ]

    def start(self):
        for copy in self.near:
            copy.start()

    def forward(self):
        for arrived, copy in zip(self.near_in, self.far):
            arrived.wait_recv()
            copy.start()

    def wait_recv(self):
        for copy in self.far_in:
            copy.wait_recv()

    def wait_send(self):
        for copy in self.near + self.far:
            copy.wait_send()


class RingScatter:
    def __init__(self, me, level, sums, far, near, send, receive):
        self.sums, self.far_slabs, self.near_slabs, self.level = sums, far, near, level
        half = sums.shape[1] // 2
        low, high = pl.ds(0, half), pl.ds(half, half)
        below, above = lax.rem(level + 3, LEVELS), lax.rem(level + 1, LEVELS)
        opposite = lax.rem(level + 2, LEVELS)

        def make(step, source, target, n):
            return hop(me, level, step, source, target, send.at[n], receive.at[n])

        self.far = [
            make(1, sums.at[opposite, low], far.at[0], 0),
            make(3, sums.at[opposite, high], far.at[1], 1),
        ]
        self.near = [
            make(1, sums.at[above], near.at[0], 2),
            make(3, sums.at[below], near.at[1], 3),
        ]
        self.places = [sums.at[above, low], sums.at[below, high]]

    def start(self):
        for copy in self.far:
            copy.start()

    def forward(self):
        for n in range(2):
            self.far[n].wait_recv()
            place = self.places[n]
            place[...] = (
                place[...].astype(F32) + self.far_slabs[n].astype(F32)
            ).astype(BF16)
            self.near[n].start()

    def result(self):
        for copy in self.near:
            copy.wait_recv()
        near = self.near_slabs
        mine = self.sums[self.level].astype(F32)
        return mine + near[0].astype(F32) + near[1].astype(F32)

    def wait_send(self):
        for copy in self.far + self.near:
            copy.wait_send()


class Spread:
    def __init__(self, me, level, source, target, send, receive):
        self.copies = []
        for step in range(1, LEVELS):
            other = lax.rem(level + step, LEVELS)
            self.copies.append(
                pltpu.make_async_remote_copy(
                    source(other),
                    target(level),
                    send.at[step],
                    receive.at[step],
                    device_id=(me, other),
                    device_id_type=MESH,
                )
            )
        self.arrivals = []
        for step in range(1, LEVELS):
            other = lax.rem(level + LEVELS - step, LEVELS)
            self.arrivals.append(
                pltpu.make_async_remote_copy(
                    source(other),
                    target(other),
                    send.at[step],
                    receive.at[step],
                    device_id=(me, other),
                    device_id_type=MESH,
                )
            )

    def start(self):
        for copy in self.copies:
            copy.start()

    def wait_recv(self):
        for copy in self.arrivals:
            copy.wait_recv()

    def wait_send(self):
        for copy in self.copies:
            copy.wait_send()


class TiledBoxes:
    def __init__(self, refs):
        self.refs = refs

    def at(self, slot, at, width):
        for ref, (start, size) in zip(self.refs, CHUNKS):
            if start <= at < start + size:
                return ref.at[slot, :, pl.ds(at - start, width)]

    def load(self, slot, at, width):
        return self.at(slot, at, width)[...].astype(F32)

    def store(self, slot, at, width, value):
        self.at(slot, at, width)[...] = value


def shift_tiles(pad, along_z, deltas, emit):
    dx, dy, dz = deltas
    start = LEFT + EDGE * dy + dz
    whole = lax.div(start, 128)
    part = start - whole * 128
    turn = lax.rem(128 - part, 128)
    lane = lax.broadcasted_iota(jnp.int32, (EDGE, 128), 1)
    from_here = lane < 128 - part
    rows = pl.ds(TOP + dx, EDGE)

    def turned(tile):
        return pltpu.roll(pad[whole + tile, rows, :], turn, 1)

    here = turned(0)
    for tile, (at, width) in enumerate(TILES):
        after = turned(tile + 1)
        out = jnp.where(from_here, here, after)
        z = along_z[:, at : at + 128] + dz
        inside = (z >= 0) & (z < EDGE)
        out = jnp.where(inside[None], out.reshape(EDGE // 8, 8, 128), 0.0).reshape(EDGE, 128)
        emit(at, width, out)
        here = after


def solve_group(me, level, group, mine, offset, partners, phis, tables, scratch, energy):
    partners, phis, returned, own_terms = [TiledBoxes(boxes) for boxes in (*partners, *phis)]
    sine_pair, plane, green, along_z = tables
    pad, den, stack, forward, scaled, inverse, shifted, potential = scratch

    def place_of(slot):
        return peer_of(me, level, div(slot, CAP)) * CAP + rem(slot, CAP)

    def deltas_of(slot):
        at = place_of(slot)
        partner, first = mine
        i = me * ORB_DEV + jnp.maximum(first[0, at], 0)
        j = peer_of(me, level, div(slot, CAP)) * ORB_DEV + jnp.maximum(partner[0, at], 0)
        return tuple(offset[axis, i] - offset[axis, j] for axis in range(3))

    def split(value):
        high = value.astype(BF16)
        return high, (value - high.astype(F32)).astype(BF16)

    def sine_product(cols):
        return jnp.dot(sine_pair[...], stack[:, cols], preferred_element_type=F32)

    def before(pair, _):
        for side in range(2):
            slot = group * BATCH + pair * 2 + side
            rows = pl.ds(pl.multiple_of(pair * 80 + side * EDGE, 8), EDGE)
            for at, width in TILES:
                pad[(LEFT + at) // 128, TOP : TOP + EDGE, :width] = partners.load(
                    slot, at, width
                )

            def emit(at, width, out):
                shifted[rows, at : at + 128] = out
                phi = phis.load(slot, at, width)
                den[side * EDGE : (side + 1) * EDGE, at : at + width] = phi * out[:, :width]

            shift_tiles(pad, along_z, deltas_of(slot), emit)
        for at, width in TILES:
            cols = slice(at, at + width)
            high, low = split(den[:, cols])
            stack[0:80, cols] = high
            stack[80:160, cols] = low
            stack[160:240, cols] = high
        rows = pl.ds(pl.multiple_of(pair * 80, 16), 80)
        for at, width in WIDE:
            cols = slice(at, at + width)
            forward[rows, cols] = sine_product(cols).astype(BF16)
        return 0

    lax.fori_loop(0, BATCH // 2, before, 0)

    def to_coeffs(step, _):
        cols = pl.ds(pl.multiple_of(step * STEP, 128), STEP)
        coeffs = jnp.dot(forward[...], plane[:, cols], preferred_element_type=F32)
        for pair in range(BATCH // 2):
            scaled[pair * 80 : pair * 80 + 80, cols] = (
                green[:, cols] * coeffs[pair * 80 : pair * 80 + 80]
            ).astype(BF16)
        return 0

    lax.fori_loop(0, PADDED // STEP, to_coeffs, 0)

    def to_inverse(step, _):
        cols = pl.ds(pl.multiple_of(step * STEP, 128), STEP)
        inverse[:, cols] = jnp.dot(
            scaled[:, :AREA], plane[:, cols], preferred_element_type=F32
        )
        return 0

    lax.fori_loop(0, PADDED // STEP, to_inverse, 0)

    def after(pair, _):
        rows = pl.ds(pl.multiple_of(pair * 80, 16), 80)
        for at, width in TILES:
            cols = slice(at, at + width)
            high, low = split(inverse[rows, cols])
            stack[0:80, cols] = high
            stack[80:160, cols] = low
            stack[160:240, cols] = high
        for at, width in WIDE:
            cols = slice(at, at + width)
            potential[:, cols] = sine_product(cols)
        for side in range(2):
            slot = group * BATCH + pair * 2 + side
            half = pl.ds(pl.multiple_of(pair * 80 + side * EDGE, 8), EDGE)
            cells = jnp.zeros((EDGE, 128), F32)
            for at, width in TILES:
                cols = slice(at, at + width)
                phi = phis.load(slot, at, width)
                solved = potential[side * EDGE : (side + 1) * EDGE, cols]
                term = solved * shifted[half, cols]
                own_terms.store(slot, at, width, term.astype(BF16))
                cell = term * phi
                if width < 128:
                    cell = jnp.concatenate([cell, jnp.zeros((EDGE, 128 - width), F32)], 1)
                cells = cells + cell
                pad[(LEFT + at) // 128, TOP : TOP + EDGE, :width] = (
                    (solved * phi).astype(BF16).astype(F32)
                )
            value = jnp.sum(jnp.sum(cells, axis=0, keepdims=True), axis=1, keepdims=True)
            lane = lax.broadcasted_iota(jnp.int32, (1, 128), 1)
            energy[...] += jnp.where(
                lane == place_of(slot), value / (EDGE * EDGE * EDGE), 0.0
            )
            back = tuple(-delta for delta in deltas_of(slot))

            def emit(at, width, out):
                returned.store(slot, at, width, out[:, :width].astype(BF16))

            shift_tiles(pad, along_z, back, emit)
        return 0

    lax.fori_loop(0, BATCH // 2, after, 0)


def add_gram(me, lists, energies, gram, half):
    orbitals = gram.shape[0]
    row = lax.broadcasted_iota(jnp.int32, (orbitals, 128), 0)
    slot = lax.broadcasted_iota(jnp.int32, (orbitals, 128), 1)
    owner_here = lax.div(row, ORB_DEV) == lax.div(slot, CAP)
    within = lax.rem(row, ORB_DEV)
    first_row = lax.broadcasted_iota(jnp.int32, (ORB_DEV, 128), 0)

    def owner(index, _):
        level, r = div(index, PEERS), rem(index, PEERS)
        here = lists[level, r]
        energy = jnp.sum(energies[level, r], axis=0)
        second = (owner_here & (within == here[0:1])).astype(F32).astype(BF16)
        value = jnp.where(first_row == here[1:2], energy, 0.0)
        high = value.astype(BF16)
        rest = value - high.astype(F32)
        middle = rest.astype(BF16)
        low = (rest - middle.astype(F32)).astype(BF16)
        parts = jnp.concatenate([high, middle, low], 0)
        out = lax.dot_general(
            parts, second, (((1,), (1,)), ((), ())), preferred_element_type=F32
        )
        rows = pl.ds(pl.multiple_of(asker_of(me, level, r) * ORB_DEV, ORB_DEV), ORB_DEV)
        half[rows, :] = out[0:32] + out[32:64] + out[64:96]
        return 0

    lax.fori_loop(0, LEVELS * PEERS, owner, 0)
    for y in range(0, orbitals, 128):
        for x in range(0, orbitals, 128):
            gram[y : y + 128, x : x + 128] = (
                half[y : y + 128, x : x + 128] + half[x : x + 128, y : y + 128].T
            )


def exchange_kernel(
    partner, first, offset, partner_row, first_row, own, sine_pair, plane_source, green,
    along_z, total_out, gram_out, *refs,
):
    count = COUNT
    gathered, picked, partners, phis, returned, far_slabs, near_slabs = [
        refs[n * count : (n + 1) * count] for n in range(7)
    ]
    sums, products, own_terms = gathered, picked, partners
    refs = refs[7 * count :]
    lists, energy, column, energies, half, plane = refs[:6]
    scratch = refs[6:14]
    total, gram, mine = refs[14:17]
    list_send, list_receive, out_send, out_receive, back_send, back_receive = refs[17:23]
    value_send, value_receive, level_send, level_receive, plane_sem, result_sem = refs[23:]
    me, level = lax.axis_index("orb"), lax.axis_index("grid")

    out, back, near, values = [], [], [], []
    for r in range(PEERS):
        block = pl.ds(r * CAP, CAP)
        asker, peer = asker_of(me, level, r), peer_of(me, level, r)
        out.append([
            Exchange(level, r, asker, picked[k].at[block], partners[k].at[block],
                     out_send.at[k, r], out_receive.at[k, r])
            for k in range(count)
        ])
        back.append([
            Exchange(level, r, peer, products[k].at[block], returned[k].at[block],
                     back_send.at[k, r], back_receive.at[k, r])
            for k in range(count)
        ])
        near.append(
            Exchange(level, r, peer, mine, lists.at[level, r],
                     list_send.at[r], list_receive.at[r])
        )
        values.append(
            Exchange(level, r, peer, column, energies.at[level, r],
                     value_send.at[r], value_receive.at[r])
        )
    gathers, scatters = [], []
    for k, (at, width) in enumerate(CHUNKS):
        gathers.append(
            RingGather(
                me, level, own.at[:, :, pl.ds(at, width)], gathered[k],
                level_send.at[k], level_receive.at[k],
            )
        )
        scatters.append(
            RingScatter(
                me, level, sums[k], far_slabs[k], near_slabs[k],
                level_send.at[count + k], level_receive.at[count + k],
            )
        )
    far = Spread(
        me, level, lambda other: lists.at[level], lambda other: lists.at[other],
        level_send.at[2 * count], level_receive.at[2 * count],
    )
    levels = Spread(
        me, level, lambda other: energy, lambda other: column.at[other],
        level_send.at[2 * count + 1], level_receive.at[2 * count + 1],
    )
    far_values = Spread(
        me, level, lambda other: energies.at[level], lambda other: energies.at[other],
        level_send.at[2 * count + 2], level_receive.at[2 * count + 2],
    )
    load_plane = pltpu.make_async_copy(plane_source, plane, plane_sem)

    load_plane.start()
    mine[0:1, :] = partner_row[...]
    mine[1:2, :] = first_row[...]
    greet(me, level)
    for copy in near:
        copy.start()
    for gather in gathers[:AHEAD]:
        gather.start()
    for k, (at, width) in enumerate(CHUNKS):
        gathered[k][level] = own[:, :, at : at + width]
    energy[...] = jnp.zeros_like(energy)
    scratch[0][...] = jnp.zeros_like(scratch[0])
    for copy in near:
        copy.wait_recv()
    far.start()

    def step_gather(k):
        if k < count:
            gathers[k].forward()
        if k + AHEAD < count:
            gathers[k + AHEAD].start()

    step_gather(0)
    asked, ahead = selectors(me, level, lists, mine)
    both = jnp.concatenate([asked, ahead], 0).astype(BF16)

    def send_out(rs, k):
        if 0 <= k < count:
            for r in rs:
                out[r][k].start()

    for k, (at, width) in enumerate(CHUNKS):
        step_gather(k + 1)
        gathers[k].wait_recv()
        planes = gathered[k].reshape(EDGE, ORB_DEV, width)
        for start in range(0, EDGE, 8):
            source = planes[start : start + 8].reshape(256, width)
            boxes = jnp.dot(both, source, preferred_element_type=F32).astype(BF16)
            boxes = boxes.reshape(2 * SLOTS, 8, width)
            picked[k][:, start : start + 8, :] = boxes[:SLOTS]
            phis[k][:, start : start + 8, :] = boxes[SLOTS:]
        for group, lag in enumerate(LAGS):
            send_out((2 * group, 2 * group + 1), k - lag)
    for k in range(count, count + max(LAGS)):
        for group, lag in enumerate(LAGS):
            send_out((2 * group, 2 * group + 1), k - lag)
    far.wait_recv()
    load_plane.wait()

    for group in range(LEVELS):
        rs = (2 * group, 2 * group + 1)
        for r in rs:
            for k in range(count):
                out[r][k].wait_recv()
                out[r][k].wait_send()
        solve_group(
            me, level, group, (partner, first), offset,
            (partners, phis), (products, own_terms),
            (sine_pair, plane, green, along_z), scratch, energy,
        )
        for k in range(count):
            if k < AT_ONCE[group]:
                for r in rs:
                    back[r][k].start()
    for gather in gathers:
        gather.wait_send()
    levels.start()
    column[level] = energy[...]
    back_select = jnp.concatenate([asked, ahead], 0).T.astype(BF16)
    levels.wait_recv()
    for copy in values:
        copy.start()
    for k, (at, width) in enumerate(CHUNKS):
        for r in range(PEERS):
            back[r][k].wait_recv()
        for r in range(PEERS):
            if AT_ONCE[r // 2] <= k + 2 < count:
                back[r][k + 2].start()
        planes = sums[k].reshape(EDGE, ORB_DEV, width)
        for start in range(0, EDGE, 8):
            rows = slice(start, start + 8)
            boxes = jnp.concatenate(
                [
                    returned[k][:, rows, :].reshape(256, width),
                    own_terms[k][:, rows, :].reshape(256, width),
                ],
                0,
            )
            slab = jnp.dot(back_select, boxes, preferred_element_type=F32)
            planes[rows] = slab.reshape(8, ORB_DEV, width).astype(BF16)
        scatters[k].start()
        if k > 0:
            scatters[k - 1].forward()
        if k == 0:
            for copy in values:
                copy.wait_recv()
            far_values.start()
    scatters[count - 1].forward()
    far_values.wait_recv()
    add_gram(me, lists, energies, gram, half)
    results = [pltpu.make_async_copy(gram, gram_out, result_sem.at[count])]
    results[0].start()
    for k, (at, width) in enumerate(CHUNKS):
        total[:, :, at : at + width] = scatters[k].result()
        cols = (slice(None), slice(None), pl.ds(at, width))
        results.append(
            pltpu.make_async_copy(total.at[cols], total_out.at[cols], result_sem.at[k])
        )
        results[-1].start()
    for copy in results:
        copy.wait()
    for copy in near + values + [copy for copies in back for copy in copies]:
        copy.wait_send()
    for spread in [far, levels, far_values] + scatters:
        spread.wait_send()


def params(mebibytes, **more):
    return pltpu.CompilerParams(vmem_limit_bytes=mebibytes * 2**20, **more)


def exchange(partner, first, offset, own):
    slab, orbitals = own.shape[0], offset.shape[1]
    constants = [jnp.asarray(table) for table in tables()]
    half_slabs = [pltpu.VMEM((2, slab // 2, ORB_DEV, width), BF16) for _, width in CHUNKS]
    two_slabs = [pltpu.VMEM((2, slab, ORB_DEV, width), BF16) for _, width in CHUNKS]
    boxes = [pltpu.VMEM((SLOTS, EDGE, width), BF16) for _, width in CHUNKS]
    slabs = [pltpu.VMEM((LEVELS, slab, ORB_DEV, width), BF16) for _, width in CHUNKS]
    any_place = pl.BlockSpec(memory_space=pl.ANY)
    dma = pltpu.SemaphoreType.DMA
    return pl.pallas_call(
        exchange_kernel,
        out_shape=(
            jax.ShapeDtypeStruct((slab, ORB_DEV, AREA), F32),
            jax.ShapeDtypeStruct((orbitals, orbitals), F32),
        ),
        in_specs=[SMEM] * 3 + [VMEM] * 4 + [any_place, VMEM, VMEM],
        out_specs=(any_place,) * 2,
        scratch_shapes=[
            *slabs, *boxes, *boxes, *boxes, *boxes, *half_slabs, *two_slabs,
            pltpu.VMEM((LEVELS, PEERS, 2, 128), jnp.int32),
            pltpu.VMEM((1, 128), F32),
            pltpu.VMEM((LEVELS, 1, 128), F32),
            pltpu.VMEM((LEVELS, PEERS, LEVELS, 1, 128), F32),
            pltpu.VMEM((orbitals, orbitals), F32),
            pltpu.VMEM((AREA, PADDED), BF16),
            pltpu.VMEM((27, 88, 128), F32),
            pltpu.VMEM((80, 1664), F32),
            pltpu.VMEM((240, AREA), BF16),
            pltpu.VMEM((BATCH * EDGE, AREA), BF16),
            pltpu.VMEM((BATCH * EDGE, PADDED), BF16),
            pltpu.VMEM((BATCH * EDGE, PADDED), F32),
            pltpu.VMEM((BATCH * EDGE, 1664), F32),
            pltpu.VMEM((80, AREA), F32),
            pltpu.VMEM((slab, ORB_DEV, AREA), F32),
            pltpu.VMEM((orbitals, orbitals), F32),
            pltpu.VMEM((2, 128), jnp.int32),
            dma((PEERS,)), dma((PEERS,)),
            dma((COUNT, PEERS)), dma((COUNT, PEERS)),
            dma((COUNT, PEERS)), dma((COUNT, PEERS)),
            dma((PEERS,)), dma((PEERS,)),
            dma((2 * COUNT + 3, LEVELS)), dma((2 * COUNT + 3, LEVELS)),
            dma(()), dma((COUNT + 1,)),
        ],
        compiler_params=params(62, collective_id=1, has_side_effects=True),
        name="exchange",
    )(partner, first, offset, partner, first, own, *constants)


def on_device(orbitals, box_offset, partner_slot, first_slot):
    terms, gram = exchange(
        partner_slot.reshape(1, -1), first_slot.reshape(1, -1), box_offset.T,
        orbitals.transpose(1, 0, 2),
    )
    return (terms.transpose(1, 0, 2), gram)


def solution(mesh):
    placed = (P("orb", "grid", None), P(), P("orb", None, None), P("orb", None, None))
    return jax.shard_map(
        on_device,
        mesh=mesh,
        in_specs=placed,
        out_specs=(P("orb", "grid", None), P()),
        check_vma=False,
    )
```

```python
import functools
import math

import jax
import jax.numpy as jnp
import ml_dtypes
import numpy as np
from jax import lax
from jax.experimental import pallas as pl
from jax.experimental.pallas import tpu as pltpu
from jax.sharding import PartitionSpec as P

BF16 = jnp.bfloat16
F32 = jnp.float32
VMEM = pl.BlockSpec(memory_space=pltpu.VMEM)
SMEM = pl.BlockSpec(memory_space=pltpu.SMEM)
EDGE = 40
AREA = 1600
ORB_DEV = 32
CAP = 4
SLOTS = 32
BATCH = 8
PADDED = 1792
STEP = 896
AHEAD = 2
LAGS = (0,0,1,2)
AT_ONCE = (6,6,3,3)
TOP = 24
LEFT = 896
TILES = [(at, min(128, AREA - at)) for at in range(0, AREA, 128)]
WIDTHS = (128, 256, 384, 384, 256, 192)
CHUNKS = [(sum(WIDTHS[:k]), width) for k, width in enumerate(WIDTHS)]
COUNT = len(CHUNKS)
PEERS = 8
LEVELS = 4
MESH = pl.DeviceIdType.MESH
WIDE = [(at, min(256, AREA - at)) for at in range(0, AREA, 256)]


@functools.cache
def tables():
    number = np.arange(EDGE, dtype=np.float64) + 1.0
    sine = np.sqrt(2.0 / (EDGE + 1.0)) * np.sin(
        math.pi * number[:, None] * number[None, :] / (EDGE + 1.0)
    )
    sine32 = sine.astype(np.float32)
    plane = (sine32[:, None, :, None] * sine32[None, :, None, :]).reshape(AREA, AREA)
    plane = np.pad(plane, ((0, 0), (0, PADDED - AREA))).astype(ml_dtypes.bfloat16)
    eigen = 2.0 - 2.0 * np.cos(math.pi * number / (EDGE + 1.0))
    green = 1.0 / (eigen[:, None, None] + eigen[None, :, None] + eigen[None, None, :])
    green = np.pad(green.reshape(EDGE, AREA), ((0, 0), (0, PADDED - AREA)))
    green = np.tile(green.astype(np.float32), (2, 1))
    high = sine32.astype(ml_dtypes.bfloat16)
    low = (sine32 - high.astype(np.float32)).astype(ml_dtypes.bfloat16)
    two = np.eye(2, dtype=np.float32)
    pair_high = np.kron(two, high.astype(np.float32))
    pair_low = np.kron(two, low.astype(np.float32))
    sine_pair = np.concatenate([pair_high, pair_high, pair_low], 1).astype(ml_dtypes.bfloat16)
    along_z = np.tile(np.arange(1664, dtype=np.int32) % EDGE, (8, 1))
    return sine_pair, plane, green, along_z


def rem(value, by):
    return value % by if isinstance(value, int) else lax.rem(value, jnp.int32(by))


def div(value, by):
    return value // by if isinstance(value, int) else lax.div(value, jnp.int32(by))


def owner_at(me, level, r, sign):
    kind = level + div(r, 4) * (3 - 2 * level)
    x = rem(div(me, 2) + 8 + sign * (2 * rem(r, 2) + rem(kind, 2)), 4)
    y = rem(div(me, 8) + 8 + sign * (2 * rem(div(r, 2), 2) + div(kind, 2)), 4)
    return y * 8 + x * 2 + rem(me + div(r, 4), 2)


def peer_of(me, level, r):
    return owner_at(me, level, r, 1)


def asker_of(me, level, r):
    return owner_at(me, level, r, -1)


def selector(index_of):
    column = lax.broadcasted_iota(jnp.int32, (8, 256), 1)
    row = lax.broadcasted_iota(jnp.int32, (8, 256), 0)
    offset = column - row * ORB_DEV
    blocks = []
    for slot in range(SLOTS):
        index = index_of(slot // CAP, slot % CAP)
        index = jnp.where(index < 0, 100000, index)
        blocks.append((offset == index).astype(F32))
    return jnp.concatenate(blocks, 0)


def entry(row, at):
    lane = lax.broadcasted_iota(jnp.int32, (1, 128), 1)
    return jnp.sum(jnp.where(lane == at, row, 0), axis=1, keepdims=True)


def selectors(me, level, lists, mine):
    asked = selector(lambda r, c: entry(lists[level, r, 0:1, :], me * CAP + c))
    ahead = selector(lambda r, c: entry(mine[1:2, :], peer_of(me, level, r) * CAP + c))
    return asked, ahead


def greet(me, level):
    barrier = pltpu.get_barrier_semaphore()
    for a in range(1, PEERS):
        pl.semaphore_signal(
            barrier, inc=1, device_id=(peer_of(me, level, a), level), device_id_type=MESH
        )
    for step in range(1, LEVELS):
        pl.semaphore_signal(
            barrier, inc=1, device_id=(me, lax.rem(level + step, LEVELS)), device_id_type=MESH
        )

    @pl.when(level != 0)
    def _():
        pl.semaphore_signal(
            barrier, inc=1, device_id=(peer_of(me, level, 0), level), device_id_type=MESH
        )
        pl.semaphore_wait(barrier, PEERS + LEVELS - 1)

    @pl.when(level == 0)
    def _():
        pl.semaphore_wait(barrier, PEERS + LEVELS - 2)


class Exchange:
    def __init__(self, level, r, owner, source, target, send, receive):
        self.level, self.r = level, r
        self.remote = pltpu.make_async_remote_copy(
            source, target, send, receive, device_id=(owner, level), device_id_type=MESH
        )
        self.local = pltpu.make_async_copy(source, target, send) if r == 0 else None

    def both(self, remote, local):
        if self.r != 0:
            remote()
            return

        pl.when(self.level != 0)(remote)
        if local is not None:
            pl.when(self.level == 0)(local)

    def start(self):
        self.both(
            lambda: self.remote.start(), lambda: self.local.start()
        )

    def wait_recv(self):
        self.both(lambda: self.remote.wait_recv(), lambda: self.local.wait())

    def wait_send(self):
        self.both(lambda: self.remote.wait_send(), None)


def hop(me, level, step, source, target, send, receive):
    return pltpu.make_async_remote_copy(
        source, target, send, receive,
        device_id=(me, lax.rem(level + step, LEVELS)), device_id_type=MESH,
    )


class RingGather:
    def __init__(self, me, level, own, gathered, send, receive):
        half = own.shape[0] // 2
        low, high = pl.ds(0, half), pl.ds(half, half)
        below, above = lax.rem(level + 3, LEVELS), lax.rem(level + 1, LEVELS)
        opposite = lax.rem(level + 2, LEVELS)

        def make(step, source, target, n):
            return hop(me, level, step, source, target, send.at[n], receive.at[n])

        self.near = [
            make(1, own, gathered.at[level], 0),
            make(3, own, gathered.at[level], 1),
        ]
        self.near_in = [
            make(1, own, gathered.at[below], 0),
            make(3, own, gathered.at[above], 1),
        ]
        self.far = [
            make(1, gathered.at[below, low], gathered.at[below, low], 2),
            make(3, gathered.at[above, high], gathered.at[above, high], 3),
        ]
        self.far_in = [
            make(1, gathered.at[below, low], gathered.at[opposite, low], 2),
            make(3, gathered.at[above, high], gathered.at[opposite, high], 3),
        ]

    def start(self):
        for copy in self.near:
            copy.start()

    def forward(self):
        for arrived, copy in zip(self.near_in, self.far):
            arrived.wait_recv()
            copy.start()

    def wait_recv(self):
        for copy in self.far_in:
            copy.wait_recv()

    def wait_send(self):
        for copy in self.near + self.far:
            copy.wait_send()


class RingScatter:
    def __init__(self, me, level, sums, far, near, send, receive):
        self.sums, self.far_slabs, self.near_slabs, self.level = sums, far, near, level
        half = sums.shape[1] // 2
        low, high = pl.ds(0, half), pl.ds(half, half)
        below, above = lax.rem(level + 3, LEVELS), lax.rem(level + 1, LEVELS)
        opposite = lax.rem(level + 2, LEVELS)

        def make(step, source, target, n):
            return hop(me, level, step, source, target, send.at[n], receive.at[n])

        self.far = [
            make(1, sums.at[opposite, low], far.at[0], 0),
            make(3, sums.at[opposite, high], far.at[1], 1),
        ]
        self.near = [
            make(1, sums.at[above], near.at[0], 2),
            make(3, sums.at[below], near.at[1], 3),
        ]
        self.places = [sums.at[above, low], sums.at[below, high]]

    def start(self):
        for copy in self.far:
            copy.start()

    def forward(self):
        for n in range(2):
            self.far[n].wait_recv()
            place = self.places[n]
            place[...] = (
                place[...].astype(F32) + self.far_slabs[n].astype(F32)
            ).astype(BF16)
            self.near[n].start()

    def result(self):
        for copy in self.near:
            copy.wait_recv()
        near = self.near_slabs
        mine = self.sums[self.level].astype(F32)
        return mine + near[0].astype(F32) + near[1].astype(F32)

    def wait_send(self):
        for copy in self.far + self.near:
            copy.wait_send()


class Spread:
    def __init__(self, me, level, source, target, send, receive):
        self.copies = []
        for step in range(1, LEVELS):
            other = lax.rem(level + step, LEVELS)
            self.copies.append(
                pltpu.make_async_remote_copy(
                    source(other),
                    target(level),
                    send.at[step],
                    receive.at[step],
                    device_id=(me, other),
                    device_id_type=MESH,
                )
            )
        self.arrivals = []
        for step in range(1, LEVELS):
            other = lax.rem(level + LEVELS - step, LEVELS)
            self.arrivals.append(
                pltpu.make_async_remote_copy(
                    source(other),
                    target(other),
                    send.at[step],
                    receive.at[step],
                    device_id=(me, other),
                    device_id_type=MESH,
                )
            )

    def start(self):
        for copy in self.copies:
            copy.start()

    def wait_recv(self):
        for copy in self.arrivals:
            copy.wait_recv()

    def wait_send(self):
        for copy in self.copies:
            copy.wait_send()


class TiledBoxes:
    def __init__(self, refs):
        self.refs = refs

    def at(self, slot, at, width):
        for ref, (start, size) in zip(self.refs, CHUNKS):
            if start <= at < start + size:
                return ref.at[slot, :, pl.ds(at - start, width)]

    def load(self, slot, at, width):
        return self.at(slot, at, width)[...].astype(F32)

    def store(self, slot, at, width, value):
        self.at(slot, at, width)[...] = value


def shift_tiles(pad, along_z, deltas, emit):
    dx, dy, dz = deltas
    start = LEFT + EDGE * dy + dz
    whole = lax.div(start, 128)
    part = start - whole * 128
    turn = lax.rem(128 - part, 128)
    lane = lax.broadcasted_iota(jnp.int32, (EDGE, 128), 1)
    from_here = lane < 128 - part
    rows = pl.ds(TOP + dx, EDGE)

    def turned(tile):
        return pltpu.roll(pad[whole + tile, rows, :], turn, 1)

    here = turned(0)
    for tile, (at, width) in enumerate(TILES):
        after = turned(tile + 1)
        out = jnp.where(from_here, here, after)
        z = along_z[:, at : at + 128] + dz
        inside = (z >= 0) & (z < EDGE)
        out = jnp.where(inside[None], out.reshape(EDGE // 8, 8, 128), 0.0).reshape(EDGE, 128)
        emit(at, width, out)
        here = after


def solve_group(me, level, group, mine, offset, partners, phis, tables, scratch, energy):
    partners, phis, returned, own_terms = [TiledBoxes(boxes) for boxes in (*partners, *phis)]
    sine_pair, plane, green, along_z = tables
    pad, den, stack, forward, scaled, inverse, shifted, potential = scratch

    def place_of(slot):
        return peer_of(me, level, div(slot, CAP)) * CAP + rem(slot, CAP)

    def deltas_of(slot):
        at = place_of(slot)
        i = me * ORB_DEV + jnp.maximum(mine[1, at], 0)
        j = peer_of(me, level, div(slot, CAP)) * ORB_DEV + jnp.maximum(mine[0, at], 0)
        return tuple(offset[axis, i] - offset[axis, j] for axis in range(3))

    def split(value):
        high = value.astype(BF16)
        return high, (value - high.astype(F32)).astype(BF16)

    def sine_product(cols):
        return jnp.dot(sine_pair[...], stack[:, cols], preferred_element_type=F32)

    def before(pair, _):
        for side in range(2):
            slot = group * BATCH + pair * 2 + side
            rows = pl.ds(pl.multiple_of(pair * 80 + side * EDGE, 8), EDGE)
            for at, width in TILES:
                pad[(LEFT + at) // 128, TOP : TOP + EDGE, :width] = partners.load(
                    slot, at, width
                )

            def emit(at, width, out):
                shifted[rows, at : at + 128] = out
                phi = phis.load(slot, at, width)
                den[side * EDGE : (side + 1) * EDGE, at : at + width] = phi * out[:, :width]

            shift_tiles(pad, along_z, deltas_of(slot), emit)
        for at, width in TILES:
            cols = slice(at, at + width)
            high, low = split(den[:, cols])
            stack[0:80, cols] = high
            stack[80:160, cols] = low
            stack[160:240, cols] = high
        rows = pl.ds(pl.multiple_of(pair * 80, 16), 80)
        for at, width in WIDE:
            cols = slice(at, at + width)
            forward[rows, cols] = sine_product(cols).astype(BF16)
        return 0

    lax.fori_loop(0, BATCH // 2, before, 0)

    def to_coeffs(step, _):
        cols = pl.ds(pl.multiple_of(step * STEP, 128), STEP)
        coeffs = jnp.dot(forward[...], plane[:, cols], preferred_element_type=F32)
        for pair in range(BATCH // 2):
            scaled[pair * 80 : pair * 80 + 80, cols] = (
                green[:, cols] * coeffs[pair * 80 : pair * 80 + 80]
            ).astype(BF16)
        return 0

    lax.fori_loop(0, PADDED // STEP, to_coeffs, 0)

    def to_inverse(step, _):
        cols = pl.ds(pl.multiple_of(step * STEP, 128), STEP)
        inverse[:, cols] = jnp.dot(
            scaled[:, :AREA], plane[:, cols], preferred_element_type=F32
        )
        return 0

    lax.fori_loop(0, PADDED // STEP, to_inverse, 0)

    def after(pair, _):
        rows = pl.ds(pl.multiple_of(pair * 80, 16), 80)
        for at, width in TILES:
            cols = slice(at, at + width)
            high, low = split(inverse[rows, cols])
            stack[0:80, cols] = high
            stack[80:160, cols] = low
            stack[160:240, cols] = high
        for at, width in WIDE:
            cols = slice(at, at + width)
            potential[:, cols] = sine_product(cols)
        for side in range(2):
            slot = group * BATCH + pair * 2 + side
            half = pl.ds(pl.multiple_of(pair * 80 + side * EDGE, 8), EDGE)
            cells = jnp.zeros((EDGE, 128), F32)
            for at, width in TILES:
                cols = slice(at, at + width)
                phi = phis.load(slot, at, width)
                solved = potential[side * EDGE : (side + 1) * EDGE, cols]
                term = solved * shifted[half, cols]
                own_terms.store(slot, at, width, term.astype(BF16))
                cell = term * phi
                if width < 128:
                    cell = jnp.concatenate([cell, jnp.zeros((EDGE, 128 - width), F32)], 1)
                cells = cells + cell
                pad[(LEFT + at) // 128, TOP : TOP + EDGE, :width] = (
                    (solved * phi).astype(BF16).astype(F32)
                )
            value = jnp.sum(jnp.sum(cells, axis=0, keepdims=True), axis=1, keepdims=True)
            lane = lax.broadcasted_iota(jnp.int32, (1, 128), 1)
            energy[...] += jnp.where(
                lane == place_of(slot), value / (EDGE * EDGE * EDGE), 0.0
            )
            back = tuple(-delta for delta in deltas_of(slot))

            def emit(at, width, out):
                returned.store(slot, at, width, out[:, :width].astype(BF16))

            shift_tiles(pad, along_z, back, emit)
        return 0

    lax.fori_loop(0, BATCH // 2, after, 0)


def add_gram(me, lists, energies, half, levels):
    orbitals = half.shape[0]
    row = lax.broadcasted_iota(jnp.int32, (orbitals, 128), 0)
    slot = lax.broadcasted_iota(jnp.int32, (orbitals, 128), 1)
    owner_here = lax.div(row, ORB_DEV) == lax.div(slot, CAP)
    within = lax.rem(row, ORB_DEV)
    first_row = lax.broadcasted_iota(jnp.int32, (ORB_DEV, 128), 0)

    def owner(index, _):
        level, r = div(index, PEERS), rem(index, PEERS)
        here = lists[level, r]
        energy = jnp.sum(energies[level, r], axis=0)
        second = (owner_here & (within == here[0:1])).astype(F32).astype(BF16)
        value = jnp.where(first_row == here[1:2], energy, 0.0)
        high = value.astype(BF16)
        rest = value - high.astype(F32)
        middle = rest.astype(BF16)
        low = (rest - middle.astype(F32)).astype(BF16)
        parts = jnp.concatenate([high, middle, low], 0)
        out = lax.dot_general(
            parts, second, (((1,), (1,)), ((), ())), preferred_element_type=F32
        )
        rows = pl.ds(pl.multiple_of(asker_of(me, level, r) * ORB_DEV, ORB_DEV), ORB_DEV)
        half[rows, :] = out[0:32] + out[32:64] + out[64:96]
        return 0

    lax.fori_loop(levels[0] * PEERS, levels[1] * PEERS, owner, 0)


def mirror_gram(gram, half):
    orbitals = gram.shape[0]
    for y in range(0, orbitals, 128):
        for x in range(0, orbitals, 128):
            gram[y : y + 128, x : x + 128] = (
                half[y : y + 128, x : x + 128] + half[x : x + 128, y : y + 128].T
            )


def exchange_kernel(
    listed, offset, mine, own, sine_pair, plane_source, green,
    along_z, total_out, gram_out, *refs,
):
    count = COUNT
    gathered, picked, partners, phis, returned, far_slabs, near_slabs = [
        refs[n * count : (n + 1) * count] for n in range(7)
    ]
    sums, products, own_terms = gathered, picked, partners
    refs = refs[7 * count :]
    lists, energy, column, energies, half, plane = refs[:6]
    scratch = refs[6:14]
    total, gram = refs[14:16]
    list_send, list_receive, out_send, out_receive, back_send, back_receive = refs[16:22]
    value_send, value_receive, level_send, level_receive, plane_sem, result_sem = refs[22:]
    me, level = lax.axis_index("orb"), lax.axis_index("grid")

    out, back, near, values = [], [], [], []
    for r in range(PEERS):
        block = pl.ds(r * CAP, CAP)
        asker, peer = asker_of(me, level, r), peer_of(me, level, r)
        out.append([
            Exchange(level, r, asker, picked[k].at[block], partners[k].at[block],
                     out_send.at[k, r], out_receive.at[k, r])
            for k in range(count)
        ])
        back.append([
            Exchange(level, r, peer, products[k].at[block], returned[k].at[block],
                     back_send.at[k, r], back_receive.at[k, r])
            for k in range(count)
        ])
        near.append(
            Exchange(level, r, peer, mine, lists.at[level, r],
                     list_send.at[r], list_receive.at[r])
        )
        values.append(
            Exchange(level, r, peer, column, energies.at[level, r],
                     value_send.at[r], value_receive.at[r])
        )
    gathers, scatters = [], []
    for k, (at, width) in enumerate(CHUNKS):
        gathers.append(
            RingGather(
                me, level, own.at[:, :, pl.ds(at, width)], gathered[k],
                level_send.at[k], level_receive.at[k],
            )
        )
        scatters.append(
            RingScatter(
                me, level, sums[k], far_slabs[k], near_slabs[k],
                level_send.at[count + k], level_receive.at[count + k],
            )
        )
    far = Spread(
        me, level, lambda other: lists.at[level], lambda other: lists.at[other],
        level_send.at[2 * count], level_receive.at[2 * count],
    )
    levels = Spread(
        me, level, lambda other: energy, lambda other: column.at[other],
        level_send.at[2 * count + 1], level_receive.at[2 * count + 1],
    )
    far_values = Spread(
        me, level, lambda other: energies.at[level], lambda other: energies.at[other],
        level_send.at[2 * count + 2], level_receive.at[2 * count + 2],
    )
    load_plane = pltpu.make_async_copy(plane_source, plane, plane_sem)

    load_plane.start()
    greet(me, level)
    for copy in near:
        copy.start()
    for gather in gathers[:AHEAD]:
        gather.start()
    for k, (at, width) in enumerate(CHUNKS):
        gathered[k][level] = own[:, :, at : at + width]
    energy[...] = jnp.zeros_like(energy)
    scratch[0][...] = jnp.zeros_like(scratch[0])
    for copy in near:
        copy.wait_recv()
    far.start()

    def step_gather(k):
        if k < count:
            gathers[k].forward()
        if k + AHEAD < count:
            gathers[k + AHEAD].start()

    step_gather(0)
    asked, ahead = selectors(me, level, lists, mine)
    both = jnp.concatenate([asked, ahead], 0).astype(BF16)

    def send_out(rs, k):
        if 0 <= k < count:
            for r in rs:
                out[r][k].start()

    for k, (at, width) in enumerate(CHUNKS):
        step_gather(k + 1)
        gathers[k].wait_recv()
        planes = gathered[k].reshape(EDGE, ORB_DEV, width)
        for start in range(0, EDGE, 8):
            source = planes[start : start + 8].reshape(256, width)
            boxes = jnp.dot(both, source, preferred_element_type=F32).astype(BF16)
            boxes = boxes.reshape(2 * SLOTS, 8, width)
            picked[k][:, start : start + 8, :] = boxes[:SLOTS]
            phis[k][:, start : start + 8, :] = boxes[SLOTS:]
        for group, lag in enumerate(LAGS):
            send_out((2 * group, 2 * group + 1), k - lag)
    for k in range(count, count + max(LAGS)):
        for group, lag in enumerate(LAGS):
            send_out((2 * group, 2 * group + 1), k - lag)
    far.wait_recv()
    load_plane.wait()

    for group in range(LEVELS):
        rs = (2 * group, 2 * group + 1)
        for r in rs:
            for k in range(count):
                out[r][k].wait_recv()
                out[r][k].wait_send()
        solve_group(
            me, level, group, listed, offset,
            (partners, phis), (products, own_terms),
            (sine_pair, plane, green, along_z), scratch, energy,
        )
        for k in range(count):
            if k < AT_ONCE[group]:
                for r in rs:
                    back[r][k].start()
    for gather in gathers:
        gather.wait_send()
    levels.start()
    column[level] = energy[...]
    results = [pltpu.make_async_copy(gram, gram_out, result_sem.at[count])]
    back_select = jnp.concatenate([asked, ahead], 0).T.astype(BF16)
    levels.wait_recv()
    for copy in values:
        copy.start()
    for k, (at, width) in enumerate(CHUNKS):
        for r in range(PEERS):
            back[r][k].wait_recv()
        for r in range(PEERS):
            if AT_ONCE[r // 2] <= k + 2 < count:
                back[r][k + 2].start()
        planes = sums[k].reshape(EDGE, ORB_DEV, width)
        for start in range(0, EDGE, 8):
            rows = slice(start, start + 8)
            boxes = jnp.concatenate(
                [
                    returned[k][:, rows, :].reshape(256, width),
                    own_terms[k][:, rows, :].reshape(256, width),
                ],
                0,
            )
            slab = jnp.dot(back_select, boxes, preferred_element_type=F32)
            planes[rows] = slab.reshape(8, ORB_DEV, width).astype(BF16)
        scatters[k].start()
        if k > 0:
            scatters[k - 1].forward()
        if k == 0:
            for copy in values:
                copy.wait_recv()
            far_values.start()
        if k == 1:
            far_values.wait_recv()
            add_gram(me, lists, energies, half, (0, 2))
        if k == 2:
            add_gram(me, lists, energies, half, (2, 4))
        if k == 3:
            mirror_gram(gram, half)
            results[0].start()
    scatters[count - 1].forward()
    for k, (at, width) in enumerate(CHUNKS):
        total[:, :, at : at + width] = scatters[k].result()
        cols = (slice(None), slice(None), pl.ds(at, width))
        results.append(
            pltpu.make_async_copy(total.at[cols], total_out.at[cols], result_sem.at[k])
        )
        results[-1].start()
    for copy in results:
        copy.wait()
    for copy in near + values + [copy for copies in back for copy in copies]:
        copy.wait_send()
    for spread in [far, levels, far_values] + scatters:
        spread.wait_send()


def params(mebibytes, **more):
    return pltpu.CompilerParams(vmem_limit_bytes=mebibytes * 2**20, **more)


def exchange(mine, offset, own):
    slab, orbitals = own.shape[0], offset.shape[1]
    constants = [jnp.asarray(table) for table in tables()]
    half_slabs = [pltpu.VMEM((2, slab // 2, ORB_DEV, width), BF16) for _, width in CHUNKS]
    two_slabs = [pltpu.VMEM((2, slab, ORB_DEV, width), BF16) for _, width in CHUNKS]
    boxes = [pltpu.VMEM((SLOTS, EDGE, width), BF16) for _, width in CHUNKS]
    slabs = [pltpu.VMEM((LEVELS, slab, ORB_DEV, width), BF16) for _, width in CHUNKS]
    any_place = pl.BlockSpec(memory_space=pl.ANY)
    dma = pltpu.SemaphoreType.DMA
    return pl.pallas_call(
        exchange_kernel,
        out_shape=(
            jax.ShapeDtypeStruct((slab, ORB_DEV, AREA), F32),
            jax.ShapeDtypeStruct((orbitals, orbitals), F32),
        ),
        in_specs=[SMEM] * 2 + [VMEM] * 3 + [any_place, VMEM, VMEM],
        out_specs=(any_place,) * 2,
        scratch_shapes=[
            *slabs, *boxes, *boxes, *boxes, *boxes, *half_slabs, *two_slabs,
            pltpu.VMEM((LEVELS, PEERS, 2, 128), jnp.int32),
            pltpu.VMEM((1, 128), F32),
            pltpu.VMEM((LEVELS, 1, 128), F32),
            pltpu.VMEM((LEVELS, PEERS, LEVELS, 1, 128), F32),
            pltpu.VMEM((orbitals, orbitals), F32),
            pltpu.VMEM((AREA, PADDED), BF16),
            pltpu.VMEM((27, 88, 128), F32),
            pltpu.VMEM((80, 1664), F32),
            pltpu.VMEM((240, AREA), BF16),
            pltpu.VMEM((BATCH * EDGE, AREA), BF16),
            pltpu.VMEM((BATCH * EDGE, PADDED), BF16),
            pltpu.VMEM((BATCH * EDGE, PADDED), F32),
            pltpu.VMEM((BATCH * EDGE, 1664), F32),
            pltpu.VMEM((80, AREA), F32),
            pltpu.VMEM((slab, ORB_DEV, AREA), F32),
            pltpu.VMEM((orbitals, orbitals), F32),
            dma((PEERS,)), dma((PEERS,)),
            dma((COUNT, PEERS)), dma((COUNT, PEERS)),
            dma((COUNT, PEERS)), dma((COUNT, PEERS)),
            dma((PEERS,)), dma((PEERS,)),
            dma((2 * COUNT + 3, LEVELS)), dma((2 * COUNT + 3, LEVELS)),
            dma(()), dma((COUNT + 1,)),
        ],
        compiler_params=params(62, collective_id=1, has_side_effects=True),
        name="exchange",
    )(mine, offset, mine, own, *constants)


def on_device(orbitals, box_offset, partner_slot, first_slot):
    terms, gram = exchange(
        jnp.concatenate([partner_slot, first_slot], 0).reshape(2, -1), box_offset.T,
        orbitals.transpose(1, 0, 2),
    )
    return (terms.transpose(1, 0, 2), gram)


def solution(mesh):
    placed = (P("orb", "grid", None), P(), P("orb", None, None), P("orb", None, None))
    return jax.shard_map(
        on_device,
        mesh=mesh,
        in_specs=placed,
        out_specs=(P("orb", "grid", None), P()),
        check_vma=False,
    )
```
